128 devices in a mesh: date: 4 (over z), row: 8 (over x, y_hi), col: 4 (over y_lo, core).
Axes of the slice: x: 4, y: 4 (y_hi: 2, y_lo: 2; y = y_hi * 2 + y_lo), z: 4, core: 2. Of those that a mesh axis runs over, the one named last changes fastest.
Arguments:
- pixels: bfloat16 [16, 64, 64, 704], P('date', 'row', 'col'), may hold values from -8 to 8
- window_query_key_value_weight: bfloat16 [704, 2112], replicated, may hold values from -1 to 1
- head_logit_scale: float32 [22], replicated, may hold values from 5 to 100
- bias_network_first: float32 [2, 512], replicated, may hold values from -4 to 4
- bias_network_second: float32 [512, 22], replicated, may hold values from -0.25 to 0.25
- window_output_weight: bfloat16 [704, 704], replicated, may hold values from -0.21875 to 0.21875
- attention_norm_gain: float32 [704], replicated, may hold values from 0.5 to 1.5
- feedforward_up_weight: bfloat16 [704, 2816], replicated, may hold values from -0.21875 to 0.21875
- feedforward_down_weight: bfloat16 [2816, 704], replicated, may hold values from -0.109375 to 0.109375
- feedforward_norm_gain: float32 [704], replicated, may hold values from 0.5 to 1.5
- temporal_norm_gain: float32 [704], replicated, may hold values from 0.5 to 8
- date_rank_embedding: float32 [16, 704], replicated, may hold values from -3 to 3
- acquisition_rank: int32 [16], replicated, may hold values from 0 to 15, each once
- temporal_query_key_value_weight: bfloat16 [704, 2112], replicated, may hold values from -1 to 1
- temporal_output_weight: bfloat16 [704, 704], replicated, may hold values from -0.21875 to 0.21875
Outputs:
- refined: bfloat16 [16, 64, 64, 704], P('date', 'row', 'col')
The draws below stay inside these ranges and needn't reach their ends.
Inputs may be any that keep to these rules, and one draw needn't show every extreme that they name: `acquisition_rank`: each of the 16 ranks appears once.
All inputs are finite; a program needn't handle non-finite values.
Results may differ from the reference program's by a relative error of at most 0.02.
Values may be sent and summed in bfloat16 or wider, within the bound.
No kernel may reach another device: no remote copies, remote signals or barrier semaphores. Data moves between devices by JAX's collectives and lax.ppermute only.
A program may use at most 192 MiB of HBM per device.

```python
import math
import jax
import jax.numpy as jnp
from jax import lax

HEAD_TOTAL = 22
C = 704
FF = 2816
BIAS_NET_UNITS = 512
WINDOW_PIXELS = 8
SHIFT = 4
DATES = 16
NH = 64
NW = 64


def tied_projection(key, features):
    raw_base = jax.random.normal(key, (features, 3 * features), jnp.float32) / math.sqrt(features)
    first_part = raw_base[:, :features]
    second_part = raw_base[:, features:2 * features]
    joined = jnp.concatenate([first_part, second_part, raw_base[:, 2 * features:]], axis=1)
    return jnp.clip(joined, -1.0, 1.0).astype(jnp.bfloat16)


def draw_pixels(key, part):
    key = jax.random.fold_in(key, 7)
    full_shape = (DATES, NH, NW, C)
    split_keys = jax.random.split(key, 4)
    pixel_scale = jnp.exp(jax.random.uniform(split_keys[3], (DATES, NH, NW, 1), jnp.float32, math.log(0.05), math.log(2.0)))
    values = jax.random.normal(split_keys[0], full_shape, jnp.float32)
    return jnp.clip(values * pixel_scale, -8.0, 8.0).astype(jnp.bfloat16)


def draw_window_query_key_value_weight(key, part):
    key = jax.random.fold_in(key, 11)
    return tied_projection(key, C)


def draw_temporal_query_key_value_weight(key, part):
    key = jax.random.fold_in(key, 13)
    return tied_projection(key, C)


def draw_head_logit_scale(key, part):
    key = jax.random.fold_in(key, 17)
    split_keys = jax.random.split(key, 1)
    upper = math.log(30.0)
    scales = jnp.exp(jax.random.uniform(split_keys[0], (HEAD_TOTAL,), jnp.float32, math.log(5.0), upper))
    return scales


def draw_temporal_norm_gain(key, part):
    key = jax.random.fold_in(key, 19)
    return jax.random.uniform(key, (C,), jnp.float32, 0.5, 1.5)


def scatter_about(key, extent, width, most, kind=jnp.bfloat16):
    values = width * jax.random.normal(key, extent, jnp.float32)
    return jnp.clip(values, min=-most, max=most).astype(kind)


def setup_inputs(seed: int = 0) -> dict:
    arg_keys = jax.random.split(jax.random.key(seed), 16)
    pixels = draw_pixels(jax.random.fold_in(arg_keys[15], 71), 0)
    window_query_key_value_weight = draw_window_query_key_value_weight(jax.random.fold_in(arg_keys[15], 71), 0)
    head_logit_scale = draw_head_logit_scale(jax.random.fold_in(arg_keys[15], 71), 0)
    bias_network_first = scatter_about(arg_keys[3], (2, BIAS_NET_UNITS), 2 ** -0.5, 4.0, jnp.float32)
    bias_network_second = scatter_about(arg_keys[4], (BIAS_NET_UNITS, HEAD_TOTAL), BIAS_NET_UNITS ** -0.5, 0.25, jnp.float32)
    window_output_weight = scatter_about(arg_keys[5], (C, C), C ** -0.5, 0.21875)
    attention_norm_gain = jnp.clip(1.0 + 0.1 * jax.random.normal(arg_keys[6], (C,), jnp.float32), 0.5, 1.5)
    feedforward_up_weight = scatter_about(arg_keys[7], (C, FF), C ** -0.5, 0.21875)
    feedforward_down_weight = scatter_about(arg_keys[8], (FF, C), FF ** -0.5, 0.109375)
    feedforward_norm_gain = jnp.clip(1.0 + 0.1 * jax.random.normal(arg_keys[9], (C,), jnp.float32), 0.5, 1.5)
    temporal_norm_gain = draw_temporal_norm_gain(jax.random.fold_in(arg_keys[15], 71), 0)
    date_rank_embedding = scatter_about(arg_keys[11], (DATES, C), 0.5, 3.0, jnp.float32)
    acquisition_rank = jax.random.permutation(arg_keys[12], DATES).astype(jnp.int32)
    temporal_query_key_value_weight = draw_temporal_query_key_value_weight(jax.random.fold_in(arg_keys[15], 71), 0)
    temporal_output_weight = scatter_about(arg_keys[14], (C, C), C ** -0.5, 0.21875)
    return {"pixels": pixels, "window_query_key_value_weight": window_query_key_value_weight, "head_logit_scale": head_logit_scale, "bias_network_first": bias_network_first, "bias_network_second": bias_network_second, "window_output_weight": window_output_weight, "attention_norm_gain": attention_norm_gain, "feedforward_up_weight": feedforward_up_weight, "feedforward_down_weight": feedforward_down_weight, "feedforward_norm_gain": feedforward_norm_gain, "temporal_norm_gain": temporal_norm_gain, "date_rank_embedding": date_rank_embedding, "acquisition_rank": acquisition_rank, "temporal_query_key_value_weight": temporal_query_key_value_weight, "temporal_output_weight": temporal_output_weight}


MASKED = -1000000000.0
FULL_PRECISION = lax.Precision.HIGHEST

def layer_norm(vector, gain_vec):
    average = lax.optimization_barrier(jnp.mean(vector, axis=-1, keepdims=True))
    centred = vector - average
    variance = lax.optimization_barrier(jnp.mean(centred * centred, axis=-1, keepdims=True))
    return centred * lax.rsqrt(variance + 1e-05) * gain_vec

def softmax_rows(scores):
    row_top = lax.optimization_barrier(jnp.max(scores, axis=-1, keepdims=True))
    exponent = jnp.exp(scores - row_top)
    return exponent / lax.optimization_barrier(jnp.sum(exponent, axis=-1, keepdims=True))

def pairwise_bias(bias_network_first, bias_network_second, window_side_length):
    window_pixel_total = window_side_length * window_side_length
    positions = jnp.arange(window_pixel_total, dtype=jnp.int32)
    row_pos = (positions // window_side_length).astype(jnp.float32)
    column_pos = (positions % window_side_length).astype(jnp.float32)
    relative_displacement = jnp.stack([row_pos[:, None] - row_pos[None, :], column_pos[:, None] - column_pos[None, :]], axis=-1)
    relative_displacement = relative_displacement * (8.0 / (window_side_length - 1))
    relative_displacement = jnp.sign(relative_displacement) * jnp.log2(jnp.abs(relative_displacement) + 1.0) / 3.0
    hidden_activation = jax.nn.relu(jnp.dot(relative_displacement.reshape(window_pixel_total * window_pixel_total, 2), bias_network_first, precision=FULL_PRECISION))
    position_bias_lookup = 16.0 * jax.nn.sigmoid(jnp.dot(hidden_activation, bias_network_second, precision=FULL_PRECISION))
    return jnp.transpose(position_bias_lookup).reshape(-1, window_pixel_total, window_pixel_total)

def band_index(coords, full_len, window_side_length):
    return (coords >= full_len - window_side_length).astype(jnp.int32) + (coords >= full_len - window_side_length // 2).astype(jnp.int32)

def partition(tile_data, window_side_length):
    batches, height, breadth, channels = tile_data.shape
    window_grid = tile_data.reshape(batches, height // window_side_length, window_side_length, breadth // window_side_length, window_side_length, channels)
    return window_grid.transpose(0, 1, 3, 2, 4, 5).reshape(-1, window_side_length * window_side_length, channels)

def unpartition(windows, batches, height, breadth, window_side_length):
    channels = windows.shape[-1]
    window_grid = windows.reshape(batches, height // window_side_length, breadth // window_side_length, window_side_length, window_side_length, channels)
    return window_grid.transpose(0, 1, 3, 2, 4, 5).reshape(batches, height, breadth, channels)

def window_attention(tile_data, regions, window_query_key_value_weight, head_logit_scale, pairwise_lookup, window_side_length):
    batches, height, breadth, features = tile_data.shape
    head_count = head_logit_scale.shape[0]
    head_size = features // head_count
    tokens = partition(tile_data, window_side_length)
    labels = partition(jnp.broadcast_to(regions[None, :, :, None], (batches, height, breadth, 1)), window_side_length)[..., 0]
    window_count = tokens.shape[0]
    window_pixel_total = window_side_length * window_side_length
    projected = jnp.dot(tokens.reshape(window_count * window_pixel_total, features), window_query_key_value_weight, preferred_element_type=jnp.float32).astype(jnp.bfloat16)
    projected = projected.reshape(window_count, window_pixel_total, 3, head_count, head_size).astype(jnp.float32)
    queries = projected[:, :, 0]
    key_vecs = projected[:, :, 1]
    values = projected[:, :, 2]
    queries = queries / jnp.maximum(jnp.sqrt(lax.optimization_barrier(jnp.sum(queries * queries, axis=-1, keepdims=True))), 1.0)
    key_vecs = key_vecs / jnp.maximum(jnp.sqrt(lax.optimization_barrier(jnp.sum(key_vecs * key_vecs, axis=-1, keepdims=True))), 1.0)
    cosine = jnp.einsum('nihd,njhd->nhij', queries, key_vecs, precision=FULL_PRECISION)
    scores = cosine * head_logit_scale[None, :, None, None] + pairwise_lookup[None]
    same_region = labels[:, None, :, None] == labels[:, None, None, :]
    scores = jnp.where(same_region, scores, MASKED)
    attn_probs = softmax_rows(scores).astype(jnp.bfloat16)
    mixed_out = jnp.einsum('nhij,njhd->nihd', attn_probs.astype(jnp.float32), values).astype(jnp.bfloat16)
    return unpartition(mixed_out.reshape(window_count, window_pixel_total, features), batches, height, breadth, window_side_length)

def settle(flat_rows, attention, window_output_weight, attention_norm_gain, feedforward_up_weight, feedforward_down_weight, feedforward_norm_gain):
    projected = jnp.dot(attention, window_output_weight, preferred_element_type=jnp.float32)
    resid = (flat_rows.astype(jnp.float32) + layer_norm(projected, attention_norm_gain)).astype(jnp.bfloat16)
    hidden_act = jax.nn.gelu(jnp.dot(resid, feedforward_up_weight, preferred_element_type=jnp.float32), approximate=False).astype(jnp.bfloat16)
    lowered = jnp.dot(hidden_act, feedforward_down_weight, preferred_element_type=jnp.float32)
    return (resid.astype(jnp.float32) + layer_norm(lowered, feedforward_norm_gain)).astype(jnp.bfloat16)

def date_inputs(block_rows, embed_rows, temporal_norm_gain, temporal_query_key_value_weight):
    features = block_rows.shape[-1]
    normed = (layer_norm(block_rows.astype(jnp.float32), temporal_norm_gain) + embed_rows[:, None, :]).astype(jnp.bfloat16)
    triple = jnp.dot(normed.reshape(-1, features), temporal_query_key_value_weight, preferred_element_type=jnp.float32).astype(jnp.bfloat16)
    return triple.reshape(block_rows.shape[0], block_rows.shape[1], 3 * features)

def date_attention(block_rows, queries, key_vecs, values, temporal_output_weight, head_count):
    dates_here, pixel_count, features = queries.shape
    head_size = features // head_count
    query_four = queries.reshape(dates_here, pixel_count, head_count, head_size).astype(jnp.float32)
    key_four = key_vecs.reshape(-1, pixel_count, head_count, head_size).astype(jnp.float32)
    value_four = values.reshape(-1, pixel_count, head_count, head_size).astype(jnp.float32)
    scores = jnp.einsum('tnhd,snhd->nhts', query_four, key_four) * head_size ** (-0.5)
    attn_probs = softmax_rows(scores).astype(jnp.bfloat16)
    attended = jnp.einsum('nhts,snhd->tnhd', attn_probs.astype(jnp.float32), value_four).astype(jnp.bfloat16)
    attended = attended.reshape(dates_here * pixel_count, features)
    lifted = jnp.dot(attended, temporal_output_weight, preferred_element_type=jnp.float32).reshape(dates_here, pixel_count, features)
    return (block_rows.astype(jnp.float32) + lifted).astype(jnp.bfloat16)

def reference(pixels, window_query_key_value_weight, head_logit_scale, bias_network_first, bias_network_second, window_output_weight, attention_norm_gain, feedforward_up_weight, feedforward_down_weight, feedforward_norm_gain, temporal_norm_gain, date_rank_embedding, acquisition_rank, temporal_query_key_value_weight, temporal_output_weight):
    pairwise_lookup = pairwise_bias(bias_network_first, bias_network_second, WINDOW_PIXELS)
    row_band = band_index(jnp.arange(NH, dtype=jnp.int32), NH, WINDOW_PIXELS)
    col_band = band_index(jnp.arange(NW, dtype=jnp.int32), NW, WINDOW_PIXELS)
    regions = 3 * row_band[:, None] + col_band[None, :]

    def per_date(frame):
        shifted = jnp.roll(frame, (-SHIFT, -SHIFT), axis=(0, 1))
        attention = window_attention(shifted[None], regions, window_query_key_value_weight, head_logit_scale, pairwise_lookup, WINDOW_PIXELS)[0]
        attention = jnp.roll(attention, (SHIFT, SHIFT), axis=(0, 1))
        mixed_out = settle(frame.reshape(NH * NW, C), attention.reshape(NH * NW, C), window_output_weight, attention_norm_gain, feedforward_up_weight, feedforward_down_weight, feedforward_norm_gain)
        return mixed_out.reshape(NH, NW, C)
    mixed_all = lax.map(per_date, pixels)
    date_embed = date_rank_embedding[acquisition_rank]
    blocks = jnp.transpose(mixed_all, (1, 0, 2, 3))

    def per_block(block_rows):
        triple = date_inputs(block_rows, date_embed, temporal_norm_gain, temporal_query_key_value_weight)
        return date_attention(block_rows, triple[..., :C], triple[..., C:2 * C], triple[..., 2 * C:], temporal_output_weight, HEAD_TOTAL)
    refined = lax.map(per_block, blocks)
    return jnp.transpose(refined, (1, 0, 2, 3))
```

```python
import functools
import math

import jax
import jax.numpy as jnp
from jax import lax
from jax.experimental import pallas as pl
from jax.experimental.pallas import tpu as pltpu
from jax.sharding import PartitionSpec as P

WINDOW = 8
SHIFT = 4
POSITIONS = WINDOW * WINDOW
PAIR = 2 * POSITIONS
MASKED = -1000000000.0
FULL_PRECISION = lax.Precision.HIGHEST
BF16 = jnp.bfloat16
F32 = jnp.float32
MIB = 1024 * 1024

VMEM = pl.BlockSpec(memory_space=pltpu.VMEM)
SMEM = pl.BlockSpec(memory_space=pltpu.SMEM)
ANY = pl.BlockSpec(memory_space=pl.ANY)


def dot(a, b):
    return jnp.dot(a, b, preferred_element_type=F32)


def dot_first(a, b):
    return lax.dot_general(a, b, (((0,), (0,)), ((), ())), preferred_element_type=F32)


def dot_last(a, b):
    return lax.dot_general(a, b, (((1,), (1,)), ((), ())), preferred_element_type=F32)


def layer_norm(vector, gain):
    average = jnp.mean(vector, axis=-1, keepdims=True)
    centred = vector - average
    variance = jnp.mean(centred * centred, axis=-1, keepdims=True)
    return centred * lax.rsqrt(variance + 1e-05) * gain


def gelu(x):
    return 0.5 * x * (1.0 + lax.erf(x * math.sqrt(0.5)))


def column_blocks(total, width):
    return [(start, min(start + width, total)) for start in range(0, total, width)]


def project(tokens, weight, queries, keys, values):
    features = weight.shape[0]
    lead = features // 128 * 128
    edge = 2 * features
    for first, last in column_blocks(weight.shape[1], 256):
        block = dot(tokens, weight[:, first:last]).astype(BF16)
        if first < features:
            stop = min(last, features)
            queries[first:stop, :] = block.T[: stop - first]
        start, stop = max(first, lead), min(last, edge)
        if start < stop:
            keys[:, start - lead : stop - lead] = block[:, start - first : stop - first]
        if last > edge:
            start = max(first, edge)
            values[start - edge : last - edge, :] = block[:, start - first :].T


def head_blocks(heads, size, features):
    offset = features % 128
    blocks = []
    for start in range(0, heads * size + offset, 128):
        blocks.append(
            [
                (h, offset + h * size - start)
                for h in range(heads)
                if start <= offset + h * size < start + 128
            ]
        )
    return blocks


def spread_queries(queries, block, size, span):
    columns = []
    for h, start in block:
        parts = [queries[h * size : (h + 1) * size, span]]
        if start:
            parts.insert(0, jnp.zeros((start, 128), BF16))
        if start + size < 128:
            parts.append(jnp.zeros((128 - size - start, 128), BF16))
        columns.append(jnp.concatenate(parts, axis=0))
    return jnp.concatenate(columns, axis=1)


def staggered(units, early, late):
    ready = early(units[0])
    for i, unit in enumerate(units):
        held = ready
        if i + 1 < len(units):
            ready = early(units[i + 1])
        late(unit, held)


def pack(pixels, low, high, low_right, high_right, work):
    dates, rows, cols, features = pixels.shape
    half = rows // 2
    for d in range(dates):
        work[...] = pixels[d].astype(F32)
        for first, out, right in ((half, low, low_right), (0, high, high_right)):
            lines = range(first, first + half)
            inner = [work[i, SHIFT : SHIFT + WINDOW, :] for i in lines]
            outer = [work[i, cols - SHIFT : cols, :] for i in lines]
            out[d] = jnp.concatenate(inner + outer, axis=0).astype(BF16)
            right[d] = jnp.concatenate([work[i, :SHIFT, :] for i in lines], axis=0).astype(BF16)


def bias_kernel(first, second, out, table):
    units = first.shape[1]
    heads = second.shape[0]
    layer = jnp.concatenate([first[...], jnp.zeros((6, units), F32)], axis=0).T
    lane = lax.broadcasted_iota(jnp.int32, (1, 128), 1)

    def mapped(offset):
        distance = offset.astype(F32) * (8.0 / (WINDOW - 1))
        size = jnp.log(jnp.abs(distance) + 1.0) * (1.0 / (3.0 * math.log(2.0)))
        return jnp.where(distance < 0, -size, size)

    row_part = layer[:, 0:1] * mapped(lax.shift_right_logical(lane, 3) - (WINDOW - 1))
    col_weight = jnp.broadcast_to(layer[:, 1:2], (units, 128))
    for col in range(WINDOW):
        hidden = jnp.maximum(row_part + col_weight * mapped((lane & 7) - col), 0.0)
        logits = jnp.dot(second[...], hidden, precision=FULL_PRECISION, preferred_element_type=F32)
        table[col * 32 : col * 32 + heads, :] = 16.0 / (1.0 + jnp.exp(-logits))
    wide = lax.broadcasted_iota(jnp.int32, (WINDOW, 128), 1)
    for h in range(heads):
        lines = table[pl.ds(h, WINDOW, stride=32), :]
        for row in range(WINDOW):
            start = (WINDOW - 1 - row) * WINDOW
            left = pltpu.roll(lines, (128 - start) % 128, 1)
            right = pltpu.roll(lines, POSITIONS - start, 1)
            out[h, row * WINDOW : (row + 1) * WINDOW, :] = jnp.where(wide < POSITIONS, left, right)


def window_kernel(straddle, *refs):
    meta, scale, low, high, *refs = refs
    if straddle:
        low_right, high_right, _, *refs = refs
    bias, qkv, lift, up, down, attention_gain, forward_gain, *refs = refs
    outs, token, refs = refs[:4], refs[4], refs[5:]
    queries, keys, low_keys, values, mixed_heads, work = refs
    features = qkv.shape[0]
    heads = bias.shape[0]
    size = features // heads
    dates = outs[0].shape[0]
    token_total = dates * POSITIONS
    half = WINDOW // 2
    inner_part = half * WINDOW
    z = meta[0]
    token[...] = jnp.zeros(token.shape, F32)
    if straddle:
        for side, (left, right) in enumerate(((low, low_right), (high, high_right))):
            for d in range(dates):
                left_rows = left[d, inner_part:, :].astype(F32)
                right_rows = right[d].astype(F32)
                for i in range(half):
                    base = d * POSITIONS + (side * half + i) * WINDOW
                    part = slice(i * SHIFT, (i + 1) * SHIFT)
                    work[base : base + SHIFT, :] = left_rows[part, :]
                    work[base + SHIFT : base + WINDOW, :] = right_rows[part, :]
        tokens = work[...].astype(BF16)
    else:
        tokens = jnp.concatenate([low[:, :inner_part], high[:, :inner_part]], axis=1)
        tokens = tokens.reshape(token_total, features)

    project(tokens, qkv, queries, keys, values)

    wide_keys = keys[...].astype(F32)
    column = lax.broadcasted_iota(jnp.int32, (wide_keys.shape[1], 128), 0) - features % 128
    owner = lax.broadcasted_iota(jnp.int32, (wide_keys.shape[1], 128), 1)
    member = jnp.where((column >= owner * size) & (column < (owner + 1) * size), 1.0, 0.0)
    member = member.astype(BF16)

    def halves(x):
        top = x.astype(BF16)
        return top, (x - top.astype(F32)).astype(BF16)

    squares, rest = halves(wide_keys * wide_keys)
    norms = dot(squares, member) + dot(rest, member)
    shrink, rest = halves(lax.rsqrt(jnp.maximum(norms, 1.0)))
    shrink = dot_last(shrink, member) + dot_last(rest, member)
    keys[...], low_keys[...] = halves(wide_keys * shrink)

    lane = lax.broadcasted_iota(jnp.int32, (POSITIONS, PAIR), 1)
    line = lax.broadcasted_iota(jnp.int32, (POSITIONS, PAIR), 0)
    first_window = lane < POSITIONS
    apart = (((lane ^ line) & 32) != 0) & (meta[1] != 0)
    if straddle:
        apart = apart | ((((lane ^ line) & 4) != 0) & (meta[2] != 0))
    closed = jnp.where(apart, MASKED, 0.0)
    keep_first = jnp.where(first_window, 1.0, 0.0).astype(BF16)
    keep_second = jnp.where(first_window, 0.0, 1.0).astype(BF16)
    blocks = head_blocks(heads, size, features)

    def early(unit):
        b, p = unit
        span = slice(p * PAIR, (p + 1) * PAIR)
        columns = slice(b * 128, (b + 1) * 128)
        left = jnp.concatenate([keys[span, columns], low_keys[span, columns]], axis=1)
        right = spread_queries(queries, blocks[b], size, span)
        return dot(left, jnp.concatenate([right, right], axis=0))

    def late(unit, both):
        b, p = unit
        span = slice(p * PAIR, (p + 1) * PAIR)
        held = []
        for i, (h, _) in enumerate(blocks[b]):
            query = queries[h * size : (h + 1) * size, span].astype(F32)
            factor = scale[h] * lax.rsqrt(
                jnp.maximum(jnp.sum(query * query, axis=0, keepdims=True), 1.0)
            )
            mine = both[:, i * PAIR : (i + 1) * PAIR]
            scores = jnp.where(first_window, mine[:POSITIONS], mine[POSITIONS:])
            scores = scores * factor + (bias[h] + closed)
            weight = jnp.exp(scores - jnp.max(scores, axis=0, keepdims=True))
            total = jnp.sum(weight, axis=0, keepdims=True)
            narrow = weight.astype(BF16)
            spread = jnp.concatenate([narrow * keep_first, narrow * keep_second], axis=0)
            held.append((h, spread, 1.0 / total))
        for h, spread, inverse in held:
            result = dot(values[h * size : (h + 1) * size, span], spread) * inverse
            mixed_heads[h * size : (h + 1) * size, span] = result.astype(BF16)

    units = [(b, p) for b in range(len(blocks)) for p in range(token_total // PAIR)]
    staggered(units, early, late)

    projected = dot_first(mixed_heads[...], lift[...])
    gain = attention_gain[...].reshape(1, features)
    resid = (tokens.astype(F32) + layer_norm(projected, gain)).astype(BF16)

    lowered = jnp.zeros((token_total, features), F32)
    for first, last in column_blocks(up.shape[1], 512):
        hidden = gelu(dot(resid, up[:, first:last])).astype(BF16)
        lowered = lowered + dot_last(hidden, down[:, first:last])
    mixed = resid.astype(F32) + layer_norm(lowered, forward_gain[...].reshape(1, features))

    part = POSITIONS // 4
    if straddle:
        work[...] = mixed
    else:
        narrow = mixed.astype(BF16).reshape(dates, 4, part, features)
    for q in range(4):
        if straddle:
            quarter = []
            for d in range(dates):
                lines = []
                for i in range(half):
                    base = d * POSITIONS + ((q // 2) * half + i) * WINDOW + (q % 2) * SHIFT
                    lines.append(work[base : base + SHIFT, :])
                quarter.append(jnp.concatenate(lines, axis=0).astype(BF16)[None])
            quarter = jnp.concatenate(quarter, axis=0)
        else:
            quarter = narrow[:, q]
        for k in range(4):

            @pl.when((z + k) % 4 == q)
            def _(quarter=quarter, k=k):
                outs[k][...] = quarter


def time_kernel(size, meta, rank, *refs):
    pieces, refs = refs[:4], refs[4:]
    _, embedding, time_gain, qkv, lift, *refs = refs
    outs, token, refs = refs[:4], refs[4], refs[5:]
    queries, keys, values, mixed_heads = refs
    features = qkv.shape[0]
    heads = features // size
    z = meta[0]
    own, pixel_count, _ = pieces[0].shape
    dates = 4 * own
    group = 128 // dates
    groups = pixel_count // group
    token[...] = jnp.zeros(token.shape, F32)

    gain = time_gain[...].reshape(1, 1, features)
    wide = []
    normed = []
    for k in range(4):
        block = pieces[k][...].astype(F32)
        source = (z + 4 - k) % 4
        lines = layer_norm(block, gain)
        for i in range(own):
            line = embedding[pl.ds(rank[source * own + i], 1), :]
            normed.append((lines[i] + line)[None])
        wide.append(block)
    normed = jnp.concatenate(normed, axis=0)
    tokens = jnp.concatenate(
        [
            normed[:, g * group : (g + 1) * group, :].reshape(128, features).astype(BF16)
            for g in range(groups)
        ],
        axis=0,
    )
    project(tokens, qkv, queries, keys, values)

    lane = lax.broadcasted_iota(jnp.int32, (group, 128), 1)
    line = lax.broadcasted_iota(jnp.int32, (group, 128), 0)
    same = jnp.where((lane & (group - 1)) == line, 1.0, 0.0)
    shrink = size ** (-0.5)
    blocks = head_blocks(heads, size, features)

    def early(unit):
        b, g = unit
        span = slice(g * 128, (g + 1) * 128)
        right = spread_queries(queries, blocks[b], size, span)
        return dot(keys[span, b * 128 : (b + 1) * 128], right)

    def late(unit, both):
        b, g = unit
        span = slice(g * 128, (g + 1) * 128)
        held = []
        for i, (h, _) in enumerate(blocks[b]):
            scores = both[:, i * 128 : (i + 1) * 128].reshape(dates, group, 128)
            weight = jnp.exp((scores - jnp.max(scores, axis=0, keepdims=True)) * shrink)
            inverse = same / jnp.sum(weight, axis=0)
            held.append((h, (weight * inverse[None]).reshape(128, 128).astype(BF16)))
        for h, probs in held:
            result = dot(values[h * size : (h + 1) * size, span], probs)
            mixed_heads[h * size : (h + 1) * size, span] = result.astype(BF16)

    units = [(b, g) for b in range(len(blocks)) for g in range(groups)]
    staggered(units, early, late)

    lifted = dot_first(mixed_heads[...], lift[...])
    for k in range(4):
        parts = [
            lifted[g * 128 : (g + 1) * 128].reshape(dates, group, features)[k * own : (k + 1) * own]
            for g in range(groups)
        ]
        outs[k][...] = (wide[k] + jnp.concatenate(parts, axis=1)).astype(BF16)


def assemble(meta, *refs):
    inner, straddle, (out, work) = refs[:4], refs[4:8], refs[8:]
    dates, rows, cols, features = out.shape
    half = rows // 2
    z = meta[0]
    for k in range(4):
        q = (z + k) % 4
        block = inner[k][...].astype(F32)
        top = (2 * q + half) % rows
        for d in range(dates):
            for j in range(2):
                work[d, top + j, SHIFT : SHIFT + WINDOW, :] = block[d, j * WINDOW : (j + 1) * WINDOW]
    for parity in range(2):

        @pl.when(z % 2 == parity)
        def _(parity=parity):
            for k in range(4):
                q = (z + k) % 4
                block = straddle[k][...].astype(F32)
                top = jnp.where(q < 2, half, 0)
                left = cols - SHIFT if (parity + k) % 2 == 0 else 0
                for d in range(dates):
                    for i in range(half):
                        work[d, top + i, left : left + SHIFT, :] = block[
                            d, i * SHIFT : (i + 1) * SHIFT
                        ]

    out[...] = work[...].astype(BF16)


def call(kernel, out_shape, in_specs, scratch, flops, moved, name, room=8):
    return pl.pallas_call(
        kernel,
        out_shape=out_shape,
        in_specs=in_specs,
        out_specs=jax.tree.map(lambda _: VMEM, out_shape),
        scratch_shapes=scratch,
        compiler_params=pltpu.CompilerParams(vmem_limit_bytes=room * MIB),
        cost_estimate=pl.CostEstimate(flops=flops, bytes_accessed=moved, transcendentals=0),
        name=name,
    )


def local(
    routes,
    pixels,
    window_query_key_value_weight,
    head_logit_scale,
    bias_network_first,
    bias_network_second,
    window_output_weight,
    attention_norm_gain,
    feedforward_up_weight,
    feedforward_down_weight,
    feedforward_norm_gain,
    temporal_norm_gain,
    date_rank_embedding,
    acquisition_rank,
    temporal_query_key_value_weight,
    temporal_output_weight,
):
    dates, rows, cols, features = pixels.shape
    heads = head_logit_scale.shape[0]
    hidden = feedforward_up_weight.shape[1]
    plane = ("row", "col")
    space = ("date", "row", "col")
    token_total = dates * POSITIONS
    part = POSITIONS // 4
    date_axis = lax.axis_size("date")
    z = lax.axis_index("date")
    last_row, last_col = routes["last"](lax.axis_index("row"), lax.axis_index("col"))
    meta = jnp.stack([z, last_row, last_col]).astype(jnp.int32)

    piece_shape = jax.ShapeDtypeStruct((dates, POSITIONS // 2 + part, features), BF16)
    part_shape = jax.ShapeDtypeStruct((dates, part, features), BF16)
    token_shape = jax.ShapeDtypeStruct((8, 128), F32)
    key_columns = -(-(features % 128 + features) // 128) * 128
    tile_bytes = pixels.size * 2

    packed = call(
        pack,
        [piece_shape] * 2 + [part_shape] * 2,
        [VMEM],
        [pltpu.VMEM(pixels.shape[1:], F32)],
        10**10,
        tile_bytes * 2,
        "pack",
    )(pixels)
    low, high, low_right, high_right = (
        lax.ppermute(piece, plane, routes[name])
        for piece, name in zip(packed, ("low", "high", "low_right", "high_right"))
    )
    bias = call(
        bias_kernel,
        jax.ShapeDtypeStruct((heads, POSITIONS, PAIR), F32),
        [VMEM, VMEM],
        [pltpu.VMEM((WINDOW * 32, 128), F32)],
        10**9,
        10**6,
        "position_bias",
    )(bias_network_first, bias_network_second.T)

    projected = [
        pltpu.VMEM((features, token_total), BF16),
        pltpu.VMEM((token_total, key_columns), BF16),
        pltpu.VMEM((token_total, key_columns), BF16),
        pltpu.VMEM((features, token_total), BF16),
        pltpu.VMEM((features, token_total), BF16),
    ]

    def window_layer(straddle, inputs):
        return call(
            functools.partial(window_kernel, straddle),
            [part_shape] * 4 + [token_shape],
            [SMEM, SMEM]
            + [VMEM] * 2
            + ([VMEM] * 2 + [ANY] if straddle else [])
            + [VMEM] * 7,
            projected + [pltpu.VMEM((token_total, features), F32)],
            2 * token_total * features * (4 * features + 2 * hidden),
            12 * 10**6,
            "window_straddle" if straddle else "window_inner",
            24,
        )(
            meta,
            head_logit_scale,
            *inputs,
            bias,
            window_query_key_value_weight,
            window_output_weight,
            feedforward_up_weight,
            feedforward_down_weight.T,
            attention_norm_gain,
            feedforward_norm_gain,
        )

    def time_layer(pieces, token):
        return call(
            functools.partial(time_kernel, features // heads),
            [part_shape] * 4 + [token_shape],
            [SMEM, SMEM] + [VMEM] * 4 + [ANY] + [VMEM] * 4,
            projected[:2] + projected[3:],
            2 * token_total * features * 4 * features,
            5 * 10**6,
            "time_layer",
            14,
        )(
            meta,
            acquisition_rank,
            *pieces,
            token,
            date_rank_embedding,
            temporal_norm_gain,
            temporal_query_key_value_weight,
            temporal_output_weight,
        )

    def to_dates(pieces, kind):
        return [lax.ppermute(piece, space, routes[kind][k]) for k, piece in enumerate(pieces)]

    def to_home(pieces):
        return [
            piece
            if k == 0
            else lax.ppermute(piece, "date", [(i, (i - k) % date_axis) for i in range(date_axis)])
            for k, piece in enumerate(pieces)
        ]

    *inner, token = window_layer(False, [low, high])
    inner = to_dates(inner, "inner")
    *straddle, token = window_layer(True, [low, high, low_right, high_right, token])
    straddle = to_dates(straddle, "straddle")
    *inner, token = time_layer(inner, token)
    inner = to_home(inner)
    *straddle, token = time_layer(straddle, token)
    straddle = to_home(straddle)
    return call(
        assemble,
        jax.ShapeDtypeStruct(pixels.shape, BF16),
        [SMEM] + [VMEM] * 8,
        [pltpu.VMEM(pixels.shape, F32)],
        0,
        tile_bytes * 2,
        "assemble",
    )(meta, *inner, *straddle)


def plan(mesh):
    dates, rows, cols = (mesh.shape[name] for name in ("date", "row", "col"))
    high, low, core = 2, cols // 2, 2
    reach = high * low

    def place(r, c):
        x, y = r // high, (r % high) * low + c // core
        y = (y + 1) % reach
        return x * high + y // low, (y % low) * core + c % core

    def flat(r, c):
        return (r % rows) * cols + c % cols

    def spot(z, r, c):
        return (z % dates) * rows * cols + flat(r, c)

    tiles = [(r, c) for r in range(rows) for c in range(cols)]

    def route(down, right):
        return [(flat(r + down, c + right), flat(*place(r, c))) for r, c in tiles]

    def forward(kind, k):
        pairs = []
        for z in range(dates):
            q = (z + k) % dates
            right = q % 2 if kind == "straddle" else 0
            for r, c in tiles:
                pairs.append((spot(z, *place(r, c)), spot(q, r + q // 2, c + right)))
        return pairs

    def last(row, col):
        y = (row % high) * low + col // core
        y = (y + reach - 1) % reach
        r = (row // high) * high + y // low
        c = (y % low) * core + col % core
        return (r == rows - 1).astype(jnp.int32), (c == cols - 1).astype(jnp.int32)

    return {
        "low": route(0, 0),
        "high": route(1, 0),
        "low_right": route(0, 1),
        "high_right": route(1, 1),
        "inner": [forward("inner", k) for k in range(dates)],
        "straddle": [forward("straddle", k) for k in range(dates)],
        "last": last,
    }


def solution(mesh):
    placed = (P("date", "row", "col", None),) + (P(),) * 14
    return jax.shard_map(
        functools.partial(local, plan(mesh)),
        mesh=mesh,
        in_specs=placed,
        out_specs=P("date", "row", "col", None),
        check_vma=False,
    )
```

```python
import functools
import math

import jax
import jax.numpy as jnp
from jax import lax
from jax.experimental import pallas as pl
from jax.experimental.pallas import tpu as pltpu
from jax.sharding import PartitionSpec as P

WINDOW = 8
SHIFT = 4
POSITIONS = WINDOW * WINDOW
PAIR = 2 * POSITIONS
MASKED = -1000000000.0
FULL_PRECISION = lax.Precision.HIGHEST
BF16 = jnp.bfloat16
F32 = jnp.float32
MIB = 1024 * 1024

VMEM = pl.BlockSpec(memory_space=pltpu.VMEM)
SMEM = pl.BlockSpec(memory_space=pltpu.SMEM)
ANY = pl.BlockSpec(memory_space=pl.ANY)


def dot(a, b):
    return jnp.dot(a, b, preferred_element_type=F32)


def dot_first(a, b):
    return lax.dot_general(a, b, (((0,), (0,)), ((), ())), preferred_element_type=F32)


def dot_last(a, b):
    return lax.dot_general(a, b, (((1,), (1,)), ((), ())), preferred_element_type=F32)


def layer_norm(vector, gain):
    average = jnp.mean(vector, axis=-1, keepdims=True)
    centred = vector - average
    variance = jnp.mean(centred * centred, axis=-1, keepdims=True)
    return centred * lax.rsqrt(variance + 1e-05) * gain


TAIL = (
    3.309271834662358e-05,
    -7.692189790236681e-04,
    8.080714484816941e-03,
    -5.3412101383958015e-02,
    -4.587709752912628e-01,
    -1.1512017013906806,
    -9.999930610827096e-01,
)


def gelu(x):
    size = jnp.abs(x)
    a = jnp.minimum(size, 6.0)
    power = TAIL[0]
    for factor in TAIL[1:]:
        power = power * a + factor
    return jnp.maximum(x, 0.0) - size * jnp.exp2(power)


def column_blocks(total, width):
    return [(start, min(start + width, total)) for start in range(0, total, width)]


def project(tokens, weight, queries, keys, values):
    features = weight.shape[0]
    lead = features // 128 * 128
    edge = 2 * features
    for first, last in column_blocks(weight.shape[1], 256):
        block = dot(tokens, weight[:, first:last]).astype(BF16)
        if first < features:
            stop = min(last, features)
            queries[first:stop, :] = block.T[: stop - first]
        start, stop = max(first, lead), min(last, edge)
        if start < stop:
            keys[:, start - lead : stop - lead] = block[:, start - first : stop - first]
        if last > edge:
            start = max(first, edge)
            values[start - edge : last - edge, :] = block[:, start - first :].T


def head_blocks(heads, size, features):
    offset = features % 128
    blocks = []
    for start in range(0, heads * size + offset, 128):
        blocks.append(
            [
                (h, offset + h * size - start)
                for h in range(heads)
                if start <= offset + h * size < start + 128
            ]
        )
    return blocks


def spread_queries(queries, block, size, span):
    columns = []
    for h, start in block:
        parts = [queries[h * size : (h + 1) * size, span]]
        if start:
            parts.insert(0, jnp.zeros((start, 128), BF16))
        if start + size < 128:
            parts.append(jnp.zeros((128 - size - start, 128), BF16))
        columns.append(jnp.concatenate(parts, axis=0))
    return jnp.concatenate(columns, axis=1)


def staggered(units, early, late):
    ready = early(units[0])
    for i, unit in enumerate(units):
        held = ready
        if i + 1 < len(units):
            ready = early(units[i + 1])
        late(unit, held)


def pack(pixels, low, high, low_right, high_right, work):
    dates, rows, cols, features = pixels.shape
    half = rows // 2
    for d in range(dates):
        work[...] = pixels[d].astype(F32)
        for first, out, right in ((half, low, low_right), (0, high, high_right)):
            lines = range(first, first + half)
            inner = [work[i, SHIFT : SHIFT + WINDOW, :] for i in lines]
            outer = [work[i, cols - SHIFT : cols, :] for i in lines]
            out[d] = jnp.concatenate(inner + outer, axis=0).astype(BF16)
            right[d] = jnp.concatenate([work[i, :SHIFT, :] for i in lines], axis=0).astype(BF16)


def bias_kernel(first, second, out, table):
    units = first.shape[1]
    heads = second.shape[0]
    layer = jnp.concatenate([first[...], jnp.zeros((6, units), F32)], axis=0).T
    lane = lax.broadcasted_iota(jnp.int32, (1, 128), 1)

    def mapped(offset):
        distance = offset.astype(F32) * (8.0 / (WINDOW - 1))
        size = jnp.log(jnp.abs(distance) + 1.0) * (1.0 / (3.0 * math.log(2.0)))
        return jnp.where(distance < 0, -size, size)

    row_part = layer[:, 0:1] * mapped(lax.shift_right_logical(lane, 3) - (WINDOW - 1))
    col_weight = jnp.broadcast_to(layer[:, 1:2], (units, 128))
    for col in range(WINDOW):
        hidden = jnp.maximum(row_part + col_weight * mapped((lane & 7) - col), 0.0)
        logits = jnp.dot(second[...], hidden, precision=FULL_PRECISION, preferred_element_type=F32)
        table[col * 32 : col * 32 + heads, :] = 16.0 / (1.0 + jnp.exp(-logits))
    wide = lax.broadcasted_iota(jnp.int32, (WINDOW, 128), 1)
    for h in range(heads):
        lines = table[pl.ds(h, WINDOW, stride=32), :]
        for row in range(WINDOW):
            start = (WINDOW - 1 - row) * WINDOW
            left = pltpu.roll(lines, (128 - start) % 128, 1)
            right = pltpu.roll(lines, POSITIONS - start, 1)
            out[h, row * WINDOW : (row + 1) * WINDOW, :] = jnp.where(wide < POSITIONS, left, right)


def inner_tokens(low, high):
    inner = WINDOW // 2 * WINDOW
    tokens = jnp.concatenate([low[:, :inner], high[:, :inner]], axis=1)
    return tokens.reshape(tokens.shape[0] * POSITIONS, tokens.shape[2])


def straddle_tokens(low_left, high_left, low_right, high_right, work):
    half = WINDOW // 2
    for side, (left, right) in enumerate(((low_left, low_right), (high_left, high_right))):
        for d in range(left.shape[0]):
            left_rows = left[d, half * WINDOW :, :].astype(F32)
            right_rows = right[d].astype(F32)
            for i in range(half):
                base = d * POSITIONS + (side * half + i) * WINDOW
                part = slice(i * SHIFT, (i + 1) * SHIFT)
                work[base : base + SHIFT, :] = left_rows[part, :]
                work[base + SHIFT : base + WINDOW, :] = right_rows[part, :]
    return work[...].astype(BF16)


def attend(tokens, last_row, last_col, scale, bias, qkv, mixed_heads, scratch):
    queries, keys, low_keys, values = scratch
    features = qkv.shape[0]
    heads = bias.shape[0]
    size = features // heads
    token_total = tokens.shape[0]
    project(tokens, qkv, queries, keys, values)

    wide_keys = keys[...].astype(F32)
    column = lax.broadcasted_iota(jnp.int32, (wide_keys.shape[1], 128), 0) - features % 128
    owner = lax.broadcasted_iota(jnp.int32, (wide_keys.shape[1], 128), 1)
    member = jnp.where((column >= owner * size) & (column < (owner + 1) * size), 1.0, 0.0)
    member = member.astype(BF16)

    def halves(x):
        top = x.astype(BF16)
        return top, (x - top.astype(F32)).astype(BF16)

    squares, rest = halves(wide_keys * wide_keys)
    norms = dot(squares, member) + dot(rest, member)
    shrink, rest = halves(lax.rsqrt(jnp.maximum(norms, 1.0)))
    shrink = dot_last(shrink, member) + dot_last(rest, member)
    keys[...], low_keys[...] = halves(wide_keys * shrink)

    lane = lax.broadcasted_iota(jnp.int32, (POSITIONS, PAIR), 1)
    line = lax.broadcasted_iota(jnp.int32, (POSITIONS, PAIR), 0)
    first_window = lane < POSITIONS
    apart = (((lane ^ line) & 32) != 0) & (last_row[0] != 0)
    if last_col is not None:
        apart = apart | ((((lane ^ line) & 4) != 0) & (last_col[0] != 0))
    closed = jnp.where(apart, MASKED, 0.0)
    keep_first = jnp.where(first_window, 1.0, 0.0).astype(BF16)
    keep_second = jnp.where(first_window, 0.0, 1.0).astype(BF16)
    blocks = head_blocks(heads, size, features)

    def early(unit):
        b, p = unit
        span = slice(p * PAIR, (p + 1) * PAIR)
        columns = slice(b * 128, (b + 1) * 128)
        left = jnp.concatenate([keys[span, columns], low_keys[span, columns]], axis=1)
        right = spread_queries(queries, blocks[b], size, span)
        return dot(left, jnp.concatenate([right, right], axis=0))

    def late(unit, both):
        b, p = unit
        span = slice(p * PAIR, (p + 1) * PAIR)
        held = []
        for i, (h, _) in enumerate(blocks[b]):
            query = queries[h * size : (h + 1) * size, span].astype(F32)
            factor = scale[h] * lax.rsqrt(
                jnp.maximum(jnp.sum(query * query, axis=0, keepdims=True), 1.0)
            )
            mine = both[:, i * PAIR : (i + 1) * PAIR]
            scores = jnp.where(first_window, mine[:POSITIONS], mine[POSITIONS:])
            scores = scores * factor + (bias[h] + closed)
            weight = jnp.exp(scores - jnp.max(scores, axis=0, keepdims=True))
            total = jnp.sum(weight, axis=0, keepdims=True)
            narrow = weight.astype(BF16)
            spread = jnp.concatenate([narrow * keep_first, narrow * keep_second], axis=0)
            held.append((h, spread, 1.0 / total))
        for h, spread, inverse in held:
            result = dot(values[h * size : (h + 1) * size, span], spread) * inverse
            mixed_heads[h * size : (h + 1) * size, span] = result.astype(BF16)

    units = [(b, p) for b in range(len(blocks)) for p in range(token_total // PAIR)]
    staggered(units, early, late)

def settle(tokens, mixed_heads, lift, up, down, attention_gain, forward_gain):
    features = tokens.shape[1]
    projected = dot_first(mixed_heads[...], lift[...])
    gain = attention_gain[...].reshape(1, features)
    resid = (tokens.astype(F32) + layer_norm(projected, gain)).astype(BF16)

    parts = []

    def raise_block(span):
        return dot(resid, up[:, slice(*span)])

    def lower_block(span, raised):
        parts.append(dot_last(gelu(raised).astype(BF16), down[:, slice(*span)]))
        if len(parts) > 1:
            parts[:] = [parts[0] + parts[1]]

    staggered(column_blocks(up.shape[1], 512), raise_block, lower_block)
    (lowered,) = parts
    return resid.astype(F32) + layer_norm(lowered, forward_gain[...].reshape(1, features))


def send_quarters(quarters, place, outs):
    for q, quarter in enumerate(quarters):
        for k in range(4):

            @pl.when((place[0] + k) % 4 == q)
            def _(quarter=quarter, k=k):
                outs[k][...] = quarter


def inner_attention(low, high, last_row, scale, bias, qkv, mixed_heads, *scratch):
    attend(inner_tokens(low, high), last_row, None, scale, bias, qkv, mixed_heads, scratch)


def inner_settle(place, low, high, mixed_heads, lift, up, down, gain, forward_gain, *outs):
    *outs, token = outs
    token[...] = jnp.zeros(token.shape, F32)
    tokens = inner_tokens(low, high)
    mixed = settle(tokens, mixed_heads, lift, up, down, gain, forward_gain)
    narrow = mixed.astype(BF16).reshape(low.shape[0], 4, POSITIONS // 4, low.shape[2])
    send_quarters([narrow[:, q] for q in range(4)], place, outs)


def straddle_window(place, last_row, last_col, scale, *refs):
    corners, _, bias, qkv, *refs = refs[:4], *refs[4:]
    lift, up, down, attention_gain, forward_gain, *refs = refs
    outs, token, scratch, mixed_heads, work = refs[:4], refs[4], refs[5:9], refs[9], refs[10]
    token[...] = jnp.zeros(token.shape, F32)
    tokens = straddle_tokens(*corners, work)
    attend(tokens, last_row, last_col, scale, bias, qkv, mixed_heads, scratch)
    work[...] = settle(tokens, mixed_heads, lift, up, down, attention_gain, forward_gain)
    half = WINDOW // 2
    quarters = []
    for q in range(4):
        quarter = []
        for d in range(corners[0].shape[0]):
            lines = []
            for i in range(half):
                base = d * POSITIONS + ((q // 2) * half + i) * WINDOW + (q % 2) * SHIFT
                lines.append(work[base : base + SHIFT, :])
            quarter.append(jnp.concatenate(lines, axis=0).astype(BF16)[None])
        quarters.append(jnp.concatenate(quarter, axis=0))
    send_quarters(quarters, place, outs)


def time_kernel(size, place, rank, *refs):
    pieces, refs = refs[:4], refs[4:]
    _, embedding, time_gain, qkv, lift, *refs = refs
    outs, token, refs = refs[:4], refs[4], refs[5:]
    queries, keys, values, mixed_heads = refs
    features = qkv.shape[0]
    heads = features // size
    z = place[0]
    own, pixel_count, _ = pieces[0].shape
    dates = 4 * own
    group = 128 // dates
    groups = pixel_count // group
    token[...] = jnp.zeros(token.shape, F32)

    gain = time_gain[...].reshape(1, 1, features)
    wide = []
    normed = []
    for k in range(4):
        block = pieces[k][...].astype(F32)
        source = (z + 4 - k) % 4
        lines = layer_norm(block, gain)
        for i in range(own):
            line = embedding[pl.ds(rank[source * own + i], 1), :]
            normed.append((lines[i] + line)[None])
        wide.append(block)
    normed = jnp.concatenate(normed, axis=0)
    tokens = jnp.concatenate(
        [
            normed[:, g * group : (g + 1) * group, :].reshape(128, features).astype(BF16)
            for g in range(groups)
        ],
        axis=0,
    )
    project(tokens, qkv, queries, keys, values)

    lane = lax.broadcasted_iota(jnp.int32, (group, 128), 1)
    line = lax.broadcasted_iota(jnp.int32, (group, 128), 0)
    same = jnp.where((lane & (group - 1)) == line, 1.0, 0.0)
    shrink = size ** (-0.5)
    blocks = head_blocks(heads, size, features)

    def early(unit):
        b, g = unit
        span = slice(g * 128, (g + 1) * 128)
        right = spread_queries(queries, blocks[b], size, span)
        return dot(keys[span, b * 128 : (b + 1) * 128], right)

    def late(unit, both):
        b, g = unit
        span = slice(g * 128, (g + 1) * 128)
        held = []
        for i, (h, _) in enumerate(blocks[b]):
            scores = both[:, i * 128 : (i + 1) * 128].reshape(dates, group, 128)
            weight = jnp.exp((scores - jnp.max(scores, axis=0, keepdims=True)) * shrink)
            inverse = same / jnp.sum(weight, axis=0)
            held.append((h, (weight * inverse[None]).reshape(128, 128).astype(BF16)))
        for h, probs in held:
            result = dot(values[h * size : (h + 1) * size, span], probs)
            mixed_heads[h * size : (h + 1) * size, span] = result.astype(BF16)

    units = [(b, g) for b in range(len(blocks)) for g in range(groups)]
    staggered(units, early, late)

    lifted = dot_first(mixed_heads[...], lift[...])
    for k in range(4):
        parts = [
            lifted[g * 128 : (g + 1) * 128].reshape(dates, group, features)[k * own : (k + 1) * own]
            for g in range(groups)
        ]
        outs[k][...] = (wide[k] + jnp.concatenate(parts, axis=1)).astype(BF16)


def assemble(place, *refs):
    inner, straddle, (out, work) = refs[:4], refs[4:8], refs[8:]
    dates, rows, cols, features = out.shape
    half = rows // 2
    z = place[0]
    for k in range(4):
        q = (z + k) % 4
        block = inner[k][...].astype(F32)
        top = (2 * q + half) % rows
        for d in range(dates):
            for j in range(2):
                work[d, top + j, SHIFT : SHIFT + WINDOW, :] = block[d, j * WINDOW : (j + 1) * WINDOW]
    for parity in range(2):

        @pl.when(z % 2 == parity)
        def _(parity=parity):
            for k in range(4):
                q = (z + k) % 4
                block = straddle[k][...].astype(F32)
                top = jnp.where(q < 2, half, 0)
                left = cols - SHIFT if (parity + k) % 2 == 0 else 0
                for d in range(dates):
                    for i in range(half):
                        work[d, top + i, left : left + SHIFT, :] = block[
                            d, i * SHIFT : (i + 1) * SHIFT
                        ]

    out[...] = work[...].astype(BF16)


def call(kernel, out_shape, in_specs, scratch, flops, moved, name, room=8):
    return pl.pallas_call(
        kernel,
        out_shape=out_shape,
        in_specs=in_specs,
        out_specs=jax.tree.map(lambda _: VMEM, out_shape),
        scratch_shapes=scratch,
        compiler_params=pltpu.CompilerParams(vmem_limit_bytes=room * MIB),
        cost_estimate=pl.CostEstimate(flops=flops, bytes_accessed=moved, transcendentals=0),
        name=name,
    )


def local(
    routes,
    pixels,
    window_query_key_value_weight,
    head_logit_scale,
    bias_network_first,
    bias_network_second,
    window_output_weight,
    attention_norm_gain,
    feedforward_up_weight,
    feedforward_down_weight,
    feedforward_norm_gain,
    temporal_norm_gain,
    date_rank_embedding,
    acquisition_rank,
    temporal_query_key_value_weight,
    temporal_output_weight,
):
    dates, rows, cols, features = pixels.shape
    heads = head_logit_scale.shape[0]
    hidden = feedforward_up_weight.shape[1]
    plane = ("row", "col")
    space = ("date", "row", "col")
    token_total = dates * POSITIONS
    part = POSITIONS // 4
    date_axis = lax.axis_size("date")
    z = lax.axis_index("date")
    last_row, last_col = routes["last"](lax.axis_index("row"), lax.axis_index("col"))
    z = z.astype(jnp.int32).reshape(1)
    last_row, last_col = last_row.reshape(1), last_col.reshape(1)

    piece_shape = jax.ShapeDtypeStruct((dates, POSITIONS // 2 + part, features), BF16)
    part_shape = jax.ShapeDtypeStruct((dates, part, features), BF16)
    token_shape = jax.ShapeDtypeStruct((8, 128), F32)
    key_columns = -(-(features % 128 + features) // 128) * 128
    tile_bytes = pixels.size * 2

    packed = call(
        pack,
        [piece_shape] * 2 + [part_shape] * 2,
        [VMEM],
        [pltpu.VMEM(pixels.shape[1:], F32)],
        10**10,
        tile_bytes * 2,
        "pack",
    )(pixels)
    low, high, low_right, high_right = (
        lax.ppermute(piece, plane, routes[name])
        for piece, name in zip(packed, ("low", "high", "low_right", "high_right"))
    )
    bias = call(
        bias_kernel,
        jax.ShapeDtypeStruct((heads, POSITIONS, PAIR), F32),
        [VMEM, VMEM],
        [pltpu.VMEM((WINDOW * 32, 128), F32)],
        10**9,
        10**6,
        "position_bias",
    )(bias_network_first, bias_network_second.T)

    projected = [
        pltpu.VMEM((features, token_total), BF16),
        pltpu.VMEM((token_total, key_columns), BF16),
        pltpu.VMEM((token_total, key_columns), BF16),
        pltpu.VMEM((features, token_total), BF16),
        pltpu.VMEM((features, token_total), BF16),
    ]

    weights = (
        window_output_weight,
        feedforward_up_weight,
        feedforward_down_weight.T,
        attention_norm_gain,
        feedforward_norm_gain,
    )
    settle_flops = 2 * token_total * features * (features + 2 * hidden)
    attend_flops = 2 * token_total * features * 3 * features * 2

    def inner_layer(low, high):
        mixed_heads = call(
            inner_attention,
            jax.ShapeDtypeStruct((features, token_total), BF16),
            [VMEM] * 2 + [SMEM] * 2 + [VMEM] * 2,
            projected[:4],
            attend_flops,
            4 * 10**6,
            "inner_attention",
            14,
        )(low, high, last_row, head_logit_scale, bias, window_query_key_value_weight)
        return call(
            inner_settle,
            [part_shape] * 4 + [token_shape],
            [SMEM] + [VMEM] * 8,
            [],
            settle_flops,
            9 * 10**6,
            "inner_settle",
            20,
        )(z, low, high, mixed_heads, *weights)

    def straddle_layer(corners, token):
        return call(
            straddle_window,
            [part_shape] * 4 + [token_shape],
            [SMEM] * 4 + [VMEM] * 4 + [ANY] + [VMEM] * 7,
            projected + [pltpu.VMEM((token_total, features), F32)],
            attend_flops + settle_flops,
            13 * 10**6,
            "straddle_window",
            24,
        )(
            z,
            last_row,
            last_col,
            head_logit_scale,
            *corners,
            token,
            bias,
            window_query_key_value_weight,
            *weights,
        )

    def time_layer(pieces, token):
        return call(
            functools.partial(time_kernel, features // heads),
            [part_shape] * 4 + [token_shape],
            [SMEM, SMEM] + [VMEM] * 4 + [ANY] + [VMEM] * 4,
            projected[:2] + projected[3:],
            2 * token_total * features * 4 * features,
            5 * 10**6,
            "time_layer",
            14,
        )(
            z,
            acquisition_rank,
            *pieces,
            token,
            date_rank_embedding,
            temporal_norm_gain,
            temporal_query_key_value_weight,
            temporal_output_weight,
        )

    def to_dates(pieces, kind):
        return [lax.ppermute(piece, space, routes[kind][k]) for k, piece in enumerate(pieces)]

    def to_home(pieces):
        return [
            piece
            if k == 0
            else lax.ppermute(piece, "date", [(i, (i - k) % date_axis) for i in range(date_axis)])
            for k, piece in enumerate(pieces)
        ]

    *inner, token = inner_layer(low, high)
    inner = to_dates(inner, "inner")
    *straddle, token = straddle_layer([low, high, low_right, high_right], token)
    straddle = to_dates(straddle, "straddle")
    *inner, token = time_layer(inner, token)
    inner = to_home(inner)
    *straddle, token = time_layer(straddle, token)
    straddle = to_home(straddle)
    return call(
        assemble,
        jax.ShapeDtypeStruct(pixels.shape, BF16),
        [SMEM] + [VMEM] * 8,
        [pltpu.VMEM(pixels.shape, F32)],
        0,
        tile_bytes * 2,
        "assemble",
    )(z, *inner, *straddle)


def plan(mesh):
    dates, rows, cols = (mesh.shape[name] for name in ("date", "row", "col"))
    high, low, core = 2, cols // 2, 2
    reach = high * low

    def place(r, c):
        x, y = r // high, (r % high) * low + c // core
        y = (y + 1) % reach
        return x * high + y // low, (y % low) * core + c % core

    def flat(r, c):
        return (r % rows) * cols + c % cols

    def spot(z, r, c):
        return (z % dates) * rows * cols + flat(r, c)

    tiles = [(r, c) for r in range(rows) for c in range(cols)]

    def route(down, right):
        return [(flat(r + down, c + right), flat(*place(r, c))) for r, c in tiles]

    def forward(kind, k):
        pairs = []
        for z in range(dates):
            q = (z + k) % dates
            right = q % 2 if kind == "straddle" else 0
            for r, c in tiles:
                pairs.append((spot(z, *place(r, c)), spot(q, r + q // 2, c + right)))
        return pairs

    def last(row, col):
        y = (row % high) * low + col // core
        y = (y + reach - 1) % reach
        r = (row // high) * high + y // low
        c = (y % low) * core + col % core
        return (r == rows - 1).astype(jnp.int32), (c == cols - 1).astype(jnp.int32)

    return {
        "low": route(0, 0),
        "high": route(1, 0),
        "low_right": route(0, 1),
        "high_right": route(1, 1),
        "inner": [forward("inner", k) for k in range(dates)],
        "straddle": [forward("straddle", k) for k in range(dates)],
        "last": last,
    }


def solution(mesh):
    placed = (P("date", "row", "col", None),) + (P(),) * 14
    return jax.shard_map(
        functools.partial(local, plan(mesh)),
        mesh=mesh,
        in_specs=placed,
        out_specs=P("date", "row", "col", None),
        check_vma=False,
    )
```

```python
import functools
import math

import jax
import jax.numpy as jnp
from jax import lax
from jax.experimental import pallas as pl
from jax.experimental.pallas import tpu as pltpu
from jax.sharding import PartitionSpec as P

WINDOW = 8
SHIFT = 4
POSITIONS = WINDOW * WINDOW
PAIR = 2 * POSITIONS
MASKED = -1000000000.0
FULL_PRECISION = lax.Precision.HIGHEST
BF16 = jnp.bfloat16
F32 = jnp.float32
MIB = 1024 * 1024

VMEM = pl.BlockSpec(memory_space=pltpu.VMEM)
SMEM = pl.BlockSpec(memory_space=pltpu.SMEM)
ANY = pl.BlockSpec(memory_space=pl.ANY)


def dot(a, b):
    return jnp.dot(a, b, preferred_element_type=F32)


def dot_first(a, b):
    return lax.dot_general(a, b, (((0,), (0,)), ((), ())), preferred_element_type=F32)


def dot_last(a, b):
    return lax.dot_general(a, b, (((1,), (1,)), ((), ())), preferred_element_type=F32)


def layer_norm(vector, gain):
    average = jnp.mean(vector, axis=-1, keepdims=True)
    centred = vector - average
    variance = jnp.mean(centred * centred, axis=-1, keepdims=True)
    return centred * lax.rsqrt(variance + 1e-05) * gain


def gelu(x):
    return 0.5 * x * (1.0 + lax.erf(x * math.sqrt(0.5)))


def column_blocks(total, width):
    return [(start, min(start + width, total)) for start in range(0, total, width)]


def project(tokens, weight, queries, keys, values):
    features = weight.shape[0]
    lead = features // 128 * 128
    edge = 2 * features
    for first, last in column_blocks(weight.shape[1], 256):
        block = dot(tokens, weight[:, first:last]).astype(BF16)
        if first < features:
            stop = min(last, features)
            queries[first:stop, :] = block.T[: stop - first]
        start, stop = max(first, lead), min(last, edge)
        if start < stop:
            keys[:, start - lead : stop - lead] = block[:, start - first : stop - first]
        if last > edge:
            start = max(first, edge)
            values[start - edge : last - edge, :] = block[:, start - first :].T


def head_blocks(heads, size, features):
    offset = features % 128
    blocks = []
    for start in range(0, heads * size + offset, 128):
        blocks.append(
            [
                (h, offset + h * size - start)
                for h in range(heads)
                if start <= offset + h * size < start + 128
            ]
        )
    return blocks


def spread_queries(queries, block, size, span):
    columns = []
    for h, start in block:
        parts = [queries[h * size : (h + 1) * size, span]]
        if start:
            parts.insert(0, jnp.zeros((start, 128), BF16))
        if start + size < 128:
            parts.append(jnp.zeros((128 - size - start, 128), BF16))
        columns.append(jnp.concatenate(parts, axis=0))
    return jnp.concatenate(columns, axis=1)


def staggered(units, early, late):
    ready = early(units[0])
    for i, unit in enumerate(units):
        held = ready
        if i + 1 < len(units):
            ready = early(units[i + 1])
        late(unit, held)


def pack(pixels, low, high, low_right, high_right, work):
    dates, rows, cols, features = pixels.shape
    half = rows // 2
    for d in range(dates):
        work[...] = pixels[d].astype(F32)
        for first, out, right in ((half, low, low_right), (0, high, high_right)):
            lines = range(first, first + half)
            inner = [work[i, SHIFT : SHIFT + WINDOW, :] for i in lines]
            outer = [work[i, cols - SHIFT : cols, :] for i in lines]
            out[d] = jnp.concatenate(inner + outer, axis=0).astype(BF16)
            right[d] = jnp.concatenate([work[i, :SHIFT, :] for i in lines], axis=0).astype(BF16)


def bias_kernel(first, second, _, out, table):
    units = first.shape[1]
    heads = second.shape[0]
    layer = jnp.concatenate([first[...], jnp.zeros((6, units), F32)], axis=0).T
    lane = lax.broadcasted_iota(jnp.int32, (1, 128), 1)

    def mapped(offset):
        distance = offset.astype(F32) * (8.0 / (WINDOW - 1))
        size = jnp.log(jnp.abs(distance) + 1.0) * (1.0 / (3.0 * math.log(2.0)))
        return jnp.where(distance < 0, -size, size)

    row_part = layer[:, 0:1] * mapped(lax.shift_right_logical(lane, 3) - (WINDOW - 1))
    col_weight = jnp.broadcast_to(layer[:, 1:2], (units, 128))
    for col in range(WINDOW):
        hidden = jnp.maximum(row_part + col_weight * mapped((lane & 7) - col), 0.0)
        logits = jnp.dot(second[...], hidden, precision=FULL_PRECISION, preferred_element_type=F32)
        table[col * 32 : col * 32 + heads, :] = 16.0 / (1.0 + jnp.exp(-logits))
    wide = lax.broadcasted_iota(jnp.int32, (WINDOW, 128), 1)
    for h in range(heads):
        lines = table[pl.ds(h, WINDOW, stride=32), :]
        for row in range(WINDOW):
            start = (WINDOW - 1 - row) * WINDOW
            left = pltpu.roll(lines, (128 - start) % 128, 1)
            right = pltpu.roll(lines, POSITIONS - start, 1)
            out[h, row * WINDOW : (row + 1) * WINDOW, :] = jnp.where(wide < POSITIONS, left, right)


def inner_tokens(low, high):
    inner = WINDOW // 2 * WINDOW
    tokens = jnp.concatenate([low[:, :inner], high[:, :inner]], axis=1)
    return tokens.reshape(tokens.shape[0] * POSITIONS, tokens.shape[2])


def straddle_tokens(low_left, high_left, low_right, high_right, work):
    half = WINDOW // 2
    for side, (left, right) in enumerate(((low_left, low_right), (high_left, high_right))):
        for d in range(left.shape[0]):
            left_rows = left[d, half * WINDOW :, :].astype(F32)
            right_rows = right[d].astype(F32)
            for i in range(half):
                base = d * POSITIONS + (side * half + i) * WINDOW
                part = slice(i * SHIFT, (i + 1) * SHIFT)
                work[base : base + SHIFT, :] = left_rows[part, :]
                work[base + SHIFT : base + WINDOW, :] = right_rows[part, :]
    return work[...].astype(BF16)


def attend(tokens, last_row, last_col, scale, bias, qkv, mixed_heads, scratch):
    queries, keys, low_keys, values = scratch
    features = qkv.shape[0]
    heads = bias.shape[0]
    size = features // heads
    token_total = tokens.shape[0]
    project(tokens, qkv, queries, keys, values)

    wide_keys = keys[...].astype(F32)
    column = lax.broadcasted_iota(jnp.int32, (wide_keys.shape[1], 128), 0) - features % 128
    owner = lax.broadcasted_iota(jnp.int32, (wide_keys.shape[1], 128), 1)
    member = jnp.where((column >= owner * size) & (column < (owner + 1) * size), 1.0, 0.0)
    member = member.astype(BF16)

    def halves(x):
        top = x.astype(BF16)
        return top, (x - top.astype(F32)).astype(BF16)

    squares, rest = halves(wide_keys * wide_keys)
    norms = dot(squares, member) + dot(rest, member)
    shrink, rest = halves(lax.rsqrt(jnp.maximum(norms, 1.0)))
    shrink = dot_last(shrink, member) + dot_last(rest, member)
    keys[...], low_keys[...] = halves(wide_keys * shrink)

    lane = lax.broadcasted_iota(jnp.int32, (POSITIONS, PAIR), 1)
    line = lax.broadcasted_iota(jnp.int32, (POSITIONS, PAIR), 0)
    first_window = lane < POSITIONS
    apart = (((lane ^ line) & 32) != 0) & (last_row[0] != 0)
    if last_col is not None:
        apart = apart | ((((lane ^ line) & 4) != 0) & (last_col[0] != 0))
    closed = jnp.where(apart, MASKED, 0.0)
    keep_first = jnp.where(first_window, 1.0, 0.0).astype(BF16)
    keep_second = jnp.where(first_window, 0.0, 1.0).astype(BF16)
    blocks = head_blocks(heads, size, features)

    def early(unit):
        b, p = unit
        span = slice(p * PAIR, (p + 1) * PAIR)
        columns = slice(b * 128, (b + 1) * 128)
        left = jnp.concatenate([keys[span, columns], low_keys[span, columns]], axis=1)
        right = spread_queries(queries, blocks[b], size, span)
        return dot(left, jnp.concatenate([right, right], axis=0))

    def late(unit, both):
        b, p = unit
        span = slice(p * PAIR, (p + 1) * PAIR)
        held = []
        for i, (h, _) in enumerate(blocks[b]):
            query = queries[h * size : (h + 1) * size, span].astype(F32)
            factor = scale[h] * lax.rsqrt(
                jnp.maximum(jnp.sum(query * query, axis=0, keepdims=True), 1.0)
            )
            mine = both[:, i * PAIR : (i + 1) * PAIR]
            scores = jnp.where(first_window, mine[:POSITIONS], mine[POSITIONS:])
            scores = scores * factor + (bias[h] + closed)
            weight = jnp.exp(scores - jnp.max(scores, axis=0, keepdims=True))
            total = jnp.sum(weight, axis=0, keepdims=True)
            narrow = weight.astype(BF16)
            spread = jnp.concatenate([narrow * keep_first, narrow * keep_second], axis=0)
            held.append((h, spread, 1.0 / total))
        for h, spread, inverse in held:
            result = dot(values[h * size : (h + 1) * size, span], spread) * inverse
            mixed_heads[h * size : (h + 1) * size, span] = result.astype(BF16)

    units = [(b, p) for b in range(len(blocks)) for p in range(token_total // PAIR)]
    staggered(units, early, late)

def settle(tokens, mixed_heads, lift, up, down, attention_gain, forward_gain):
    features = tokens.shape[1]
    projected = dot_first(mixed_heads, lift[...])
    gain = attention_gain[...].reshape(1, features)
    resid = (tokens.astype(F32) + layer_norm(projected, gain)).astype(BF16)

    parts = []

    def raise_block(span):
        return dot(resid, up[:, slice(*span)])

    def lower_block(span, raised):
        parts.append(dot_last(gelu(raised).astype(BF16), down[:, slice(*span)]))
        if len(parts) > 1:
            parts[:] = [parts[0] + parts[1]]

    staggered(column_blocks(up.shape[1], 512), raise_block, lower_block)
    (lowered,) = parts
    return resid.astype(F32) + layer_norm(lowered, forward_gain[...].reshape(1, features))


def send_quarters(quarters, place, outs):
    for q, quarter in enumerate(quarters):
        for k in range(4):

            @pl.when((place[0] + k) % 4 == q)
            def _(quarter=quarter, k=k):
                outs[k][...] = quarter


def inner_attention(low, high, last_row, scale, bias, qkv, mixed_heads, *scratch):
    attend(inner_tokens(low, high), last_row, None, scale, bias, qkv, mixed_heads, scratch)


def straddle_attention(*refs):
    corners, (_, last_row, last_col, scale, bias, qkv, mixed_heads) = refs[:4], refs[4:11]
    *scratch, work = refs[11:]
    tokens = straddle_tokens(*corners, work)
    attend(tokens, last_row, last_col, scale, bias, qkv, mixed_heads, scratch)


def settle_all(place, *refs):
    corners, (inner_heads, straddle_heads, *weights), refs = refs[:4], refs[4:11], refs[11:]
    outs, token, work = refs[:4], refs[4], refs[5]
    token[...] = jnp.zeros(token.shape, F32)
    dates, _, features = corners[0].shape
    half = WINDOW // 2
    inner_total = dates * POSITIONS
    tokens = jnp.concatenate(
        [inner_tokens(*corners[:2]), straddle_tokens(*corners, work)], axis=0
    )
    mixed_heads = jnp.concatenate([inner_heads[...], straddle_heads[...]], axis=1)
    mixed = settle(tokens, mixed_heads, *weights)
    work[...] = mixed[inner_total:]
    narrow = mixed[:inner_total].astype(BF16).reshape(dates, 4, POSITIONS // 4, features)
    quarters = []
    for q in range(4):
        quarter = []
        for d in range(dates):
            lines = []
            for i in range(half):
                base = d * POSITIONS + ((q // 2) * half + i) * WINDOW + (q % 2) * SHIFT
                lines.append(work[base : base + SHIFT, :])
            quarter.append(jnp.concatenate(lines, axis=0).astype(BF16)[None])
        quarters.append(jnp.concatenate([narrow[:, q], jnp.concatenate(quarter, axis=0)], axis=1))
    send_quarters(quarters, place, outs)


def time_kernel(size, pixel_start, place, rank, *refs):
    pieces, refs = refs[:4], refs[4:]
    _, embedding, time_gain, qkv, lift, *refs = refs
    outs, token, refs = refs[:4], refs[4], refs[5:]
    queries, keys, values, mixed_heads = refs
    features = qkv.shape[0]
    heads = features // size
    z = place[0]
    own, pixel_count, _ = outs[0].shape
    dates = 4 * own
    group = 128 // dates
    groups = pixel_count // group
    token[...] = jnp.zeros(token.shape, F32)

    gain = time_gain[...].reshape(1, 1, features)
    wide = []
    normed = []
    for k in range(4):
        block = pieces[k][:, pixel_start : pixel_start + pixel_count, :].astype(F32)
        source = (z + 4 - k) % 4
        lines = layer_norm(block, gain)
        for i in range(own):
            line = embedding[pl.ds(rank[source * own + i], 1), :]
            normed.append((lines[i] + line)[None])
        wide.append(block)
    normed = jnp.concatenate(normed, axis=0)
    tokens = jnp.concatenate(
        [
            normed[:, g * group : (g + 1) * group, :].reshape(128, features).astype(BF16)
            for g in range(groups)
        ],
        axis=0,
    )
    project(tokens, qkv, queries, keys, values)

    lane = lax.broadcasted_iota(jnp.int32, (group, 128), 1)
    line = lax.broadcasted_iota(jnp.int32, (group, 128), 0)
    same = jnp.where((lane & (group - 1)) == line, 1.0, 0.0)
    shrink = size ** (-0.5)
    blocks = head_blocks(heads, size, features)

    def early(unit):
        b, g = unit
        span = slice(g * 128, (g + 1) * 128)
        right = spread_queries(queries, blocks[b], size, span)
        return dot(keys[span, b * 128 : (b + 1) * 128], right)

    def late(unit, both):
        b, g = unit
        span = slice(g * 128, (g + 1) * 128)
        held = []
        for i, (h, _) in enumerate(blocks[b]):
            scores = both[:, i * 128 : (i + 1) * 128].reshape(dates, group, 128)
            weight = jnp.exp((scores - jnp.max(scores, axis=0, keepdims=True)) * shrink)
            inverse = same / jnp.sum(weight, axis=0)
            held.append((h, (weight * inverse[None]).reshape(128, 128).astype(BF16)))
        for h, probs in held:
            result = dot(values[h * size : (h + 1) * size, span], probs)
            mixed_heads[h * size : (h + 1) * size, span] = result.astype(BF16)

    units = [(b, g) for b in range(len(blocks)) for g in range(groups)]
    staggered(units, early, late)

    lifted = dot_first(mixed_heads[...], lift[...])
    for k in range(4):
        parts = [
            lifted[g * 128 : (g + 1) * 128].reshape(dates, group, features)[k * own : (k + 1) * own]
            for g in range(groups)
        ]
        outs[k][...] = (wide[k] + jnp.concatenate(parts, axis=1)).astype(BF16)


def assemble(place, *refs):
    inner, straddle, (out, work) = refs[:4], refs[4:8], refs[8:]
    dates, rows, cols, features = out.shape
    half = rows // 2
    z = place[0]
    for k in range(4):
        q = (z + k) % 4
        block = inner[k][...].astype(F32)
        top = (2 * q + half) % rows
        for d in range(dates):
            for j in range(2):
                work[d, top + j, SHIFT : SHIFT + WINDOW, :] = block[d, j * WINDOW : (j + 1) * WINDOW]
    for parity in range(2):

        @pl.when(z % 2 == parity)
        def _(parity=parity):
            for k in range(4):
                q = (z + k) % 4
                block = straddle[k][...].astype(F32)
                top = jnp.where(q < 2, half, 0)
                left = cols - SHIFT if (parity + k) % 2 == 0 else 0
                for d in range(dates):
                    for i in range(half):
                        work[d, top + i, left : left + SHIFT, :] = block[
                            d, i * SHIFT : (i + 1) * SHIFT
                        ]

    out[...] = work[...].astype(BF16)


def call(kernel, out_shape, in_specs, scratch, flops, moved, name, room=8):
    return pl.pallas_call(
        kernel,
        out_shape=out_shape,
        in_specs=in_specs,
        out_specs=jax.tree.map(lambda _: VMEM, out_shape),
        scratch_shapes=scratch,
        compiler_params=pltpu.CompilerParams(vmem_limit_bytes=room * MIB),
        cost_estimate=pl.CostEstimate(flops=flops, bytes_accessed=moved, transcendentals=0),
        name=name,
    )


def local(
    routes,
    pixels,
    window_query_key_value_weight,
    head_logit_scale,
    bias_network_first,
    bias_network_second,
    window_output_weight,
    attention_norm_gain,
    feedforward_up_weight,
    feedforward_down_weight,
    feedforward_norm_gain,
    temporal_norm_gain,
    date_rank_embedding,
    acquisition_rank,
    temporal_query_key_value_weight,
    temporal_output_weight,
):
    dates, rows, cols, features = pixels.shape
    heads = head_logit_scale.shape[0]
    hidden = feedforward_up_weight.shape[1]
    plane = ("row", "col")
    space = ("date", "row", "col")
    token_total = dates * POSITIONS
    part = POSITIONS // 4
    z = lax.axis_index("date")
    last_row, last_col = routes["last"](lax.axis_index("row"), lax.axis_index("col"))
    z = z.astype(jnp.int32).reshape(1)
    last_row, last_col = last_row.reshape(1), last_col.reshape(1)

    piece_shape = jax.ShapeDtypeStruct((dates, POSITIONS // 2 + part, features), BF16)
    part_shape = jax.ShapeDtypeStruct((dates, part, features), BF16)
    token_shape = jax.ShapeDtypeStruct((8, 128), F32)
    key_columns = -(-(features % 128 + features) // 128) * 128
    tile_bytes = pixels.size * 2

    packed = call(
        pack,
        [piece_shape] * 2 + [part_shape] * 2,
        [VMEM],
        [pltpu.VMEM(pixels.shape[1:], F32)],
        10**10,
        tile_bytes * 2,
        "pack",
    )(pixels)
    low, high, low_right, high_right = (
        lax.ppermute(piece, plane, routes[name])
        for piece, name in zip(packed, ("low", "high", "low_right", "high_right"))
    )
    bias = call(
        bias_kernel,
        jax.ShapeDtypeStruct((heads, POSITIONS, PAIR), F32),
        [VMEM] * 3,
        [pltpu.VMEM((WINDOW * 32, 128), F32)],
        10**9,
        10**6,
        "position_bias",
    )(bias_network_first, bias_network_second.T, window_query_key_value_weight)

    projected = [
        pltpu.VMEM((features, token_total), BF16),
        pltpu.VMEM((token_total, key_columns), BF16),
        pltpu.VMEM((token_total, key_columns), BF16),
        pltpu.VMEM((features, token_total), BF16),
        pltpu.VMEM((features, token_total), BF16),
    ]

    weights = (
        window_output_weight,
        feedforward_up_weight,
        feedforward_down_weight.T,
        attention_norm_gain,
        feedforward_norm_gain,
    )
    settle_flops = 2 * token_total * features * (features + 2 * hidden)
    attend_flops = 2 * token_total * features * 3 * features * 2

    heads_shape = jax.ShapeDtypeStruct((features, token_total), BF16)
    attention = (head_logit_scale, bias, window_query_key_value_weight)
    work = pltpu.VMEM((token_total, features), F32)

    def window_layer(low, high, *rights):
        inner_heads = call(
            inner_attention,
            heads_shape,
            [VMEM] * 2 + [SMEM] * 2 + [VMEM] * 2,
            projected[:4],
            attend_flops,
            4 * 10**6,
            "inner_attention",
            14,
        )(low, high, last_row, *attention)
        straddle_heads = call(
            straddle_attention,
            heads_shape,
            [VMEM] * 4 + [ANY] + [SMEM] * 3 + [VMEM] * 2,
            projected[:4] + [work],
            attend_flops,
            4 * 10**6,
            "straddle_attention",
            14,
        )(low, high, *rights, inner_heads, last_row, last_col, *attention)
        return call(
            settle_all,
            [jax.ShapeDtypeStruct((dates, 2 * part, features), BF16)] * 4 + [token_shape],
            [SMEM] + [VMEM] * 11,
            [work],
            2 * settle_flops,
            9 * 10**6,
            "settle",
            28,
        )(z, low, high, *rights, inner_heads, straddle_heads, *weights)

    def time_layer(pixel_start, pieces, token):
        return call(
            functools.partial(time_kernel, features // heads, pixel_start),
            [part_shape] * 4 + [token_shape],
            [SMEM, SMEM] + [VMEM] * 4 + [ANY] + [VMEM] * 4,
            projected[:2] + projected[3:],
            2 * token_total * features * 4 * features,
            5 * 10**6,
            "time_layer",
            14,
        )(
            z,
            acquisition_rank,
            *pieces,
            token,
            date_rank_embedding,
            temporal_norm_gain,
            temporal_query_key_value_weight,
            temporal_output_weight,
        )

    def moved(pieces, kind):
        return [lax.ppermute(piece, space, route) for piece, route in zip(pieces, routes[kind])]

    *mixed, token = window_layer(low, high, low_right, high_right)
    mixed = moved(mixed, "forward")
    *inner, token = time_layer(0, mixed, token)
    inner = inner[:1] + moved(inner[1:], "inner")
    *straddle, token = time_layer(part, mixed, token)
    straddle = moved(straddle, "straddle")
    return call(
        assemble,
        jax.ShapeDtypeStruct(pixels.shape, BF16),
        [SMEM] + [VMEM] * 8,
        [pltpu.VMEM(pixels.shape, F32)],
        0,
        tile_bytes * 2,
        "assemble",
    )(z, *inner, *straddle)


def plan(mesh):
    dates, rows, cols = (mesh.shape[name] for name in ("date", "row", "col"))
    high, low, core = 2, cols // 2, 2
    reach = high * low

    def place(r, c):
        x, y = r // high, (r % high) * low + c // core
        y = (y + 1) % reach
        return x * high + y // low, (y % low) * core + c % core

    def flat(r, c):
        return (r % rows) * cols + c % cols

    def spot(z, r, c):
        return (z % dates) * rows * cols + flat(r, c)

    tiles = [(r, c) for r in range(rows) for c in range(cols)]

    def route(down, right):
        return [(flat(r + down, c + right), flat(*place(r, c))) for r, c in tiles]

    spots = [(z, r, c) for z in range(dates) for r, c in tiles]

    def forward(k):
        pairs = []
        for z, r, c in spots:
            q = (z + k) % dates
            pairs.append((spot(z, *place(r, c)), spot(q, r + q // 2, c)))
        return pairs

    def back(k, right):
        return [(spot(z, r, c), spot(z - k, r, c + right * (z % 2))) for z, r, c in spots]

    def last(row, col):
        y = (row % high) * low + col // core
        y = (y + reach - 1) % reach
        r = (row // high) * high + y // low
        c = (y % low) * core + col % core
        return (r == rows - 1).astype(jnp.int32), (c == cols - 1).astype(jnp.int32)

    return {
        "low": route(0, 0),
        "high": route(1, 0),
        "low_right": route(0, 1),
        "high_right": route(1, 1),
        "forward": [forward(k) for k in range(dates)],
        "inner": [back(k, 0) for k in range(1, dates)],
        "straddle": [back(k, 1) for k in range(dates)],
        "last": last,
    }


def solution(mesh):
    placed = (P("date", "row", "col", None),) + (P(),) * 14
    return jax.shard_map(
        functools.partial(local, plan(mesh)),
        mesh=mesh,
        in_specs=placed,
        out_specs=P("date", "row", "col", None),
        check_vma=False,
    )
```

```python
import functools
import math

import jax
import jax.numpy as jnp
from jax import lax
from jax.experimental import pallas as pl
from jax.experimental.pallas import tpu as pltpu
from jax.sharding import PartitionSpec as P

WINDOW = 8
SHIFT = 4
POSITIONS = WINDOW * WINDOW
PAIR = 2 * POSITIONS
MASKED = -1000000000.0
FULL_PRECISION = lax.Precision.HIGHEST
BF16 = jnp.bfloat16
F32 = jnp.float32
MIB = 1024 * 1024

VMEM = pl.BlockSpec(memory_space=pltpu.VMEM)
SMEM = pl.BlockSpec(memory_space=pltpu.SMEM)
ANY = pl.BlockSpec(memory_space=pl.ANY)


def dot(a, b):
    return jnp.dot(a, b, preferred_element_type=F32)


def dot_first(a, b):
    return lax.dot_general(a, b, (((0,), (0,)), ((), ())), preferred_element_type=F32)


def dot_last(a, b):
    return lax.dot_general(a, b, (((1,), (1,)), ((), ())), preferred_element_type=F32)


def layer_norm(vector, gain):
    average = jnp.mean(vector, axis=-1, keepdims=True)
    centred = vector - average
    variance = jnp.mean(centred * centred, axis=-1, keepdims=True)
    return centred * lax.rsqrt(variance + 1e-05) * gain


def gelu(x):
    return 0.5 * x * (1.0 + lax.erf(x * math.sqrt(0.5)))


def column_blocks(total, width):
    return [(start, min(start + width, total)) for start in range(0, total, width)]


def project(tokens, weight, queries, keys, values):
    features = weight.shape[0]
    lead = features // 128 * 128
    edge = 2 * features
    for first, last in column_blocks(weight.shape[1], 256):
        block = dot(tokens, weight[:, first:last]).astype(BF16)
        if first < features:
            stop = min(last, features)
            queries[first:stop, :] = block.T[: stop - first]
        start, stop = max(first, lead), min(last, edge)
        if start < stop:
            keys[:, start - lead : stop - lead] = block[:, start - first : stop - first]
        if last > edge:
            start = max(first, edge)
            values[start - edge : last - edge, :] = block[:, start - first :].T


def head_blocks(heads, size, features):
    offset = features % 128
    blocks = []
    for start in range(0, heads * size + offset, 128):
        blocks.append(
            [
                (h, offset + h * size - start)
                for h in range(heads)
                if start <= offset + h * size < start + 128
            ]
        )
    return blocks


def spread_queries(queries, block, size, span):
    columns = []
    for h, start in block:
        parts = [queries[h * size : (h + 1) * size, span]]
        if start:
            parts.insert(0, jnp.zeros((start, 128), BF16))
        if start + size < 128:
            parts.append(jnp.zeros((128 - size - start, 128), BF16))
        columns.append(jnp.concatenate(parts, axis=0))
    return jnp.concatenate(columns, axis=1)


def staggered(units, early, late):
    ready = early(units[0])
    for i, unit in enumerate(units):
        held = ready
        if i + 1 < len(units):
            ready = early(units[i + 1])
        late(unit, held)


def pack(pixels, low, high, low_right, high_right, work):
    dates, rows, cols, features = pixels.shape
    half = rows // 2
    for d in range(dates):
        work[...] = pixels[d].astype(F32)
        for first, out, right in ((half, low, low_right), (0, high, high_right)):
            lines = range(first, first + half)
            inner = [work[i, SHIFT : SHIFT + WINDOW, :] for i in lines]
            outer = [work[i, cols - SHIFT : cols, :] for i in lines]
            out[d] = jnp.concatenate(inner + outer, axis=0).astype(BF16)
            right[d] = jnp.concatenate([work[i, :SHIFT, :] for i in lines], axis=0).astype(BF16)


def bias_kernel(first, second, _, out, table):
    units = first.shape[1]
    heads = second.shape[0]
    layer = jnp.concatenate([first[...], jnp.zeros((6, units), F32)], axis=0).T
    lane = lax.broadcasted_iota(jnp.int32, (1, 128), 1)

    def mapped(offset):
        distance = offset.astype(F32) * (8.0 / (WINDOW - 1))
        size = jnp.log(jnp.abs(distance) + 1.0) * (1.0 / (3.0 * math.log(2.0)))
        return jnp.where(distance < 0, -size, size)

    row_part = layer[:, 0:1] * mapped(lax.shift_right_logical(lane, 3) - (WINDOW - 1))
    col_weight = jnp.broadcast_to(layer[:, 1:2], (units, 128))
    for col in range(WINDOW):
        hidden = jnp.maximum(row_part + col_weight * mapped((lane & 7) - col), 0.0)
        logits = jnp.dot(second[...], hidden, precision=FULL_PRECISION, preferred_element_type=F32)
        table[col * 32 : col * 32 + heads, :] = 16.0 / (1.0 + jnp.exp(-logits))
    wide = lax.broadcasted_iota(jnp.int32, (WINDOW, 128), 1)
    for h in range(heads):
        lines = table[pl.ds(h, WINDOW, stride=32), :]
        for row in range(WINDOW):
            start = (WINDOW - 1 - row) * WINDOW
            left = pltpu.roll(lines, (128 - start) % 128, 1)
            right = pltpu.roll(lines, POSITIONS - start, 1)
            out[h, row * WINDOW : (row + 1) * WINDOW, :] = jnp.where(wide < POSITIONS, left, right)


def inner_tokens(low, high):
    inner = WINDOW // 2 * WINDOW
    tokens = jnp.concatenate([low[:, :inner], high[:, :inner]], axis=1)
    return tokens.reshape(tokens.shape[0] * POSITIONS, tokens.shape[2])


def straddle_tokens(low_left, high_left, low_right, high_right, work):
    half = WINDOW // 2
    for side, (left, right) in enumerate(((low_left, low_right), (high_left, high_right))):
        for d in range(left.shape[0]):
            left_rows = left[d, half * WINDOW :, :].astype(F32)
            right_rows = right[d].astype(F32)
            for i in range(half):
                base = d * POSITIONS + (side * half + i) * WINDOW
                part = slice(i * SHIFT, (i + 1) * SHIFT)
                work[base : base + SHIFT, :] = left_rows[part, :]
                work[base + SHIFT : base + WINDOW, :] = right_rows[part, :]
    return work[...].astype(BF16)


def attend(tokens, last_row, last_col, scale, bias, qkv, mixed_heads, scratch):
    queries, keys, low_keys, values = scratch
    features = qkv.shape[0]
    heads = bias.shape[0]
    size = features // heads
    token_total = tokens.shape[0]
    project(tokens, qkv, queries, keys, values)

    wide_keys = keys[...].astype(F32)
    column = lax.broadcasted_iota(jnp.int32, (wide_keys.shape[1], 128), 0) - features % 128
    owner = lax.broadcasted_iota(jnp.int32, (wide_keys.shape[1], 128), 1)
    member = jnp.where((column >= owner * size) & (column < (owner + 1) * size), 1.0, 0.0)
    member = member.astype(BF16)

    def halves(x):
        top = x.astype(BF16)
        return top, (x - top.astype(F32)).astype(BF16)

    squares, rest = halves(wide_keys * wide_keys)
    norms = dot(squares, member) + dot(rest, member)
    shrink, rest = halves(lax.rsqrt(jnp.maximum(norms, 1.0)))
    shrink = dot_last(shrink, member) + dot_last(rest, member)
    keys[...], low_keys[...] = halves(wide_keys * shrink)

    lane = lax.broadcasted_iota(jnp.int32, (POSITIONS, PAIR), 1)
    line = lax.broadcasted_iota(jnp.int32, (POSITIONS, PAIR), 0)
    first_window = lane < POSITIONS
    apart = (((lane ^ line) & 32) != 0) & (last_row[0] != 0)
    if last_col is not None:
        apart = apart | ((((lane ^ line) & 4) != 0) & (last_col[0] != 0))
    closed = jnp.where(apart, MASKED, 0.0)
    keep_first = jnp.where(first_window, 1.0, 0.0).astype(BF16)
    keep_second = jnp.where(first_window, 0.0, 1.0).astype(BF16)
    blocks = head_blocks(heads, size, features)

    def early(unit):
        b, p = unit
        span = slice(p * PAIR, (p + 1) * PAIR)
        columns = slice(b * 128, (b + 1) * 128)
        left = jnp.concatenate([keys[span, columns], low_keys[span, columns]], axis=1)
        right = spread_queries(queries, blocks[b], size, span)
        return dot(left, jnp.concatenate([right, right], axis=0))

    def late(unit, both):
        b, p = unit
        span = slice(p * PAIR, (p + 1) * PAIR)
        held = []
        for i, (h, _) in enumerate(blocks[b]):
            query = queries[h * size : (h + 1) * size, span].astype(F32)
            factor = scale[h] * lax.rsqrt(
                jnp.maximum(jnp.sum(query * query, axis=0, keepdims=True), 1.0)
            )
            mine = both[:, i * PAIR : (i + 1) * PAIR]
            scores = jnp.where(first_window, mine[:POSITIONS], mine[POSITIONS:])
            scores = scores * factor + (bias[h] + closed)
            weight = jnp.exp(scores - jnp.max(scores, axis=0, keepdims=True))
            total = jnp.sum(weight, axis=0, keepdims=True)
            narrow = weight.astype(BF16)
            spread = jnp.concatenate([narrow * keep_first, narrow * keep_second], axis=0)
            held.append((h, spread, 1.0 / total))
        for h, spread, inverse in held:
            result = dot(values[h * size : (h + 1) * size, span], spread) * inverse
            mixed_heads[h * size : (h + 1) * size, span] = result.astype(BF16)

    units = [(b, p) for b in range(len(blocks)) for p in range(token_total // PAIR)]
    staggered(units, early, late)

def settle(tokens, mixed_heads, lift, up, down, attention_gain, forward_gain):
    features = tokens.shape[1]
    projected = dot_first(mixed_heads[...], lift[...])
    gain = attention_gain[...].reshape(1, features)
    resid = (tokens.astype(F32) + layer_norm(projected, gain)).astype(BF16)

    total = up.shape[1]
    raised, parts = [], []

    def raise_block(span):
        return dot(resid, up[:, slice(*span)])

    def lower_block(span, block):
        raised.append(gelu(block).astype(BF16))
        if len(raised) == 2 or span[1] == total:
            start = span[1] - 256 * len(raised)
            hidden = jnp.concatenate(raised, axis=1)
            parts.append(dot_last(hidden, down[:, start : span[1]]))
            raised.clear()
            if len(parts) > 1:
                parts[:] = [parts[0] + parts[1]]

    staggered(column_blocks(total, 256), raise_block, lower_block)
    (lowered,) = parts
    return resid.astype(F32) + layer_norm(lowered, forward_gain[...].reshape(1, features))


def send_quarters(quarters, place, outs):
    for q, quarter in enumerate(quarters):
        for k in range(4):

            @pl.when((place[0] + k) % 4 == q)
            def _(quarter=quarter, k=k):
                outs[k][...] = quarter


def inner_attention(low, high, last_row, scale, bias, qkv, mixed_heads, *scratch):
    attend(inner_tokens(low, high), last_row, None, scale, bias, qkv, mixed_heads, scratch)


def inner_settle(place, low, high, mixed_heads, lift, up, down, gain, forward_gain, *outs):
    *outs, token = outs
    token[...] = jnp.zeros(token.shape, F32)
    tokens = inner_tokens(low, high)
    mixed = settle(tokens, mixed_heads, lift, up, down, gain, forward_gain)
    narrow = mixed.astype(BF16).reshape(low.shape[0], 4, POSITIONS // 4, low.shape[2])
    send_quarters([narrow[:, q] for q in range(4)], place, outs)


def straddle_window(place, last_row, last_col, scale, *refs):
    corners, _, bias, qkv, *refs = refs[:4], *refs[4:]
    lift, up, down, attention_gain, forward_gain, *refs = refs
    outs, token, scratch, mixed_heads, work = refs[:4], refs[4], refs[5:9], refs[9], refs[10]
    token[...] = jnp.zeros(token.shape, F32)
    tokens = straddle_tokens(*corners, work)
    attend(tokens, last_row, last_col, scale, bias, qkv, mixed_heads, scratch)
    work[...] = settle(tokens, mixed_heads, lift, up, down, attention_gain, forward_gain)
    half = WINDOW // 2
    quarters = []
    for q in range(4):
        quarter = []
        for d in range(corners[0].shape[0]):
            lines = []
            for i in range(half):
                base = d * POSITIONS + ((q // 2) * half + i) * WINDOW + (q % 2) * SHIFT
                lines.append(work[base : base + SHIFT, :])
            quarter.append(jnp.concatenate(lines, axis=0).astype(BF16)[None])
        quarters.append(jnp.concatenate(quarter, axis=0))
    send_quarters(quarters, place, outs)


def time_kernel(size, place, rank, *refs):
    pieces, refs = refs[:4], refs[4:]
    _, embedding, time_gain, qkv, lift, *refs = refs
    outs, token, refs = refs[:4], refs[4], refs[5:]
    queries, keys, values, mixed_heads = refs
    features = qkv.shape[0]
    heads = features // size
    z = place[0]
    own, pixel_count, _ = pieces[0].shape
    dates = 4 * own
    group = 128 // dates
    groups = pixel_count // group
    token[...] = jnp.zeros(token.shape, F32)

    gain = time_gain[...].reshape(1, 1, features)
    wide = []
    normed = []
    for k in range(4):
        block = pieces[k][...].astype(F32)
        source = (z + 4 - k) % 4
        lines = layer_norm(block, gain)
        for i in range(own):
            line = embedding[pl.ds(rank[source * own + i], 1), :]
            normed.append((lines[i] + line)[None])
        wide.append(block)
    normed = jnp.concatenate(normed, axis=0)
    tokens = jnp.concatenate(
        [
            normed[:, g * group : (g + 1) * group, :].reshape(128, features).astype(BF16)
            for g in range(groups)
        ],
        axis=0,
    )
    project(tokens, qkv, queries, keys, values)

    lane = lax.broadcasted_iota(jnp.int32, (group, 128), 1)
    line = lax.broadcasted_iota(jnp.int32, (group, 128), 0)
    same = jnp.where((lane & (group - 1)) == line, 1.0, 0.0)
    shrink = size ** (-0.5)
    blocks = head_blocks(heads, size, features)

    def early(unit):
        b, g = unit
        span = slice(g * 128, (g + 1) * 128)
        right = spread_queries(queries, blocks[b], size, span)
        return dot(keys[span, b * 128 : (b + 1) * 128], right)

    def late(unit, both):
        b, g = unit
        span = slice(g * 128, (g + 1) * 128)
        held = []
        for i, (h, _) in enumerate(blocks[b]):
            scores = both[:, i * 128 : (i + 1) * 128].reshape(dates, group, 128)
            weight = jnp.exp((scores - jnp.max(scores, axis=0, keepdims=True)) * shrink)
            inverse = same / jnp.sum(weight, axis=0)
            held.append((h, (weight * inverse[None]).reshape(128, 128).astype(BF16)))
        for h, probs in held:
            result = dot(values[h * size : (h + 1) * size, span], probs)
            mixed_heads[h * size : (h + 1) * size, span] = result.astype(BF16)

    units = [(b, g) for b in range(len(blocks)) for g in range(groups)]
    staggered(units, early, late)

    lifted = dot_first(mixed_heads[...], lift[...])
    for k in range(4):
        parts = [
            lifted[g * 128 : (g + 1) * 128].reshape(dates, group, features)[k * own : (k + 1) * own]
            for g in range(groups)
        ]
        outs[k][...] = (wide[k] + jnp.concatenate(parts, axis=1)).astype(BF16)


def assemble(place, *refs):
    inner, straddle, (out, work) = refs[:4], refs[4:8], refs[8:]
    dates, rows, cols, features = out.shape
    half = rows // 2
    z = place[0]
    for k in range(4):
        q = (z + k) % 4
        block = inner[k][...].astype(F32)
        top = (2 * q + half) % rows
        for d in range(dates):
            for j in range(2):
                work[d, top + j, SHIFT : SHIFT + WINDOW, :] = block[d, j * WINDOW : (j + 1) * WINDOW]
    for parity in range(2):

        @pl.when(z % 2 == parity)
        def _(parity=parity):
            for k in range(4):
                q = (z + k) % 4
                block = straddle[k][...].astype(F32)
                top = jnp.where(q < 2, half, 0)
                left = cols - SHIFT if (parity + k) % 2 == 0 else 0
                for d in range(dates):
                    for i in range(half):
                        work[d, top + i, left : left + SHIFT, :] = block[
                            d, i * SHIFT : (i + 1) * SHIFT
                        ]

    out[...] = work[...].astype(BF16)


def call(kernel, out_shape, in_specs, scratch, flops, moved, name, room=8):
    return pl.pallas_call(
        kernel,
        out_shape=out_shape,
        in_specs=in_specs,
        out_specs=jax.tree.map(lambda _: VMEM, out_shape),
        scratch_shapes=scratch,
        compiler_params=pltpu.CompilerParams(vmem_limit_bytes=room * MIB),
        cost_estimate=pl.CostEstimate(flops=flops, bytes_accessed=moved, transcendentals=0),
        name=name,
    )


def local(
    routes,
    pixels,
    window_query_key_value_weight,
    head_logit_scale,
    bias_network_first,
    bias_network_second,
    window_output_weight,
    attention_norm_gain,
    feedforward_up_weight,
    feedforward_down_weight,
    feedforward_norm_gain,
    temporal_norm_gain,
    date_rank_embedding,
    acquisition_rank,
    temporal_query_key_value_weight,
    temporal_output_weight,
):
    dates, rows, cols, features = pixels.shape
    heads = head_logit_scale.shape[0]
    hidden = feedforward_up_weight.shape[1]
    plane = ("row", "col")
    space = ("date", "row", "col")
    token_total = dates * POSITIONS
    part = POSITIONS // 4
    date_axis = lax.axis_size("date")
    z = lax.axis_index("date")
    last_row, last_col = routes["last"](lax.axis_index("row"), lax.axis_index("col"))
    z = z.astype(jnp.int32).reshape(1)
    last_row, last_col = last_row.reshape(1), last_col.reshape(1)

    piece_shape = jax.ShapeDtypeStruct((dates, POSITIONS // 2 + part, features), BF16)
    part_shape = jax.ShapeDtypeStruct((dates, part, features), BF16)
    token_shape = jax.ShapeDtypeStruct((8, 128), F32)
    key_columns = -(-(features % 128 + features) // 128) * 128
    tile_bytes = pixels.size * 2

    packed = call(
        pack,
        [piece_shape] * 2 + [part_shape] * 2,
        [VMEM],
        [pltpu.VMEM(pixels.shape[1:], F32)],
        10**10,
        tile_bytes * 2,
        "pack",
        4,
    )(pixels)
    low, high, low_right, high_right = (
        lax.ppermute(piece, plane, routes[name])
        for piece, name in zip(packed, ("low", "high", "low_right", "high_right"))
    )
    bias = call(
        bias_kernel,
        jax.ShapeDtypeStruct((heads, POSITIONS, PAIR), F32),
        [VMEM] * 3,
        [pltpu.VMEM((WINDOW * 32, 128), F32)],
        10**9,
        10**6,
        "position_bias",
        6,
    )(bias_network_first, bias_network_second.T, window_query_key_value_weight)

    projected = [
        pltpu.VMEM((features, token_total), BF16),
        pltpu.VMEM((token_total, key_columns), BF16),
        pltpu.VMEM((token_total, key_columns), BF16),
        pltpu.VMEM((features, token_total), BF16),
        pltpu.VMEM((features, token_total), BF16),
    ]

    weights = (
        window_output_weight,
        feedforward_up_weight,
        feedforward_down_weight.T,
        attention_norm_gain,
        feedforward_norm_gain,
    )
    settle_flops = 2 * token_total * features * (features + 2 * hidden)
    attend_flops = 2 * token_total * features * 3 * features * 2

    def inner_layer(low, high):
        mixed_heads = call(
            inner_attention,
            jax.ShapeDtypeStruct((features, token_total), BF16),
            [VMEM] * 2 + [SMEM] * 2 + [VMEM] * 2,
            projected[:4],
            attend_flops,
            4 * 10**6,
            "inner_attention",
            14,
        )(low, high, last_row, head_logit_scale, bias, window_query_key_value_weight)
        return call(
            inner_settle,
            [part_shape] * 4 + [token_shape],
            [SMEM] + [VMEM] * 8,
            [],
            settle_flops,
            9 * 10**6,
            "inner_settle",
            20,
        )(z, low, high, mixed_heads, *weights)

    def straddle_layer(corners, token):
        return call(
            straddle_window,
            [part_shape] * 4 + [token_shape],
            [SMEM] * 4 + [VMEM] * 4 + [ANY] + [VMEM] * 7,
            projected + [pltpu.VMEM((token_total, features), F32)],
            attend_flops + settle_flops,
            13 * 10**6,
            "straddle_window",
            24,
        )(
            z,
            last_row,
            last_col,
            head_logit_scale,
            *corners,
            token,
            bias,
            window_query_key_value_weight,
            *weights,
        )

    def time_layer(pieces, token):
        return call(
            functools.partial(time_kernel, features // heads),
            [part_shape] * 4 + [token_shape],
            [SMEM, SMEM] + [VMEM] * 4 + [ANY] + [VMEM] * 4,
            projected[:2] + projected[3:],
            2 * token_total * features * 4 * features,
            5 * 10**6,
            "time_layer",
            14,
        )(
            z,
            acquisition_rank,
            *pieces,
            token,
            date_rank_embedding,
            temporal_norm_gain,
            temporal_query_key_value_weight,
            temporal_output_weight,
        )

    def to_dates(pieces, kind):
        return [lax.ppermute(piece, space, routes[kind][k]) for k, piece in enumerate(pieces)]

    def to_home(pieces):
        return [
            piece
            if k == 0
            else lax.ppermute(piece, "date", [(i, (i - k) % date_axis) for i in range(date_axis)])
            for k, piece in enumerate(pieces)
        ]

    *inner, token = inner_layer(low, high)
    inner = to_dates(inner, "inner")
    *straddle, token = straddle_layer([low, high, low_right, high_right], token)
    straddle = to_dates(straddle, "straddle")
    *inner, token = time_layer(inner, token)
    inner = to_home(inner)
    *straddle, token = time_layer(straddle, token)
    straddle = to_home(straddle)
    return call(
        assemble,
        jax.ShapeDtypeStruct(pixels.shape, BF16),
        [SMEM] + [VMEM] * 8,
        [pltpu.VMEM(pixels.shape, F32)],
        0,
        tile_bytes * 2,
        "assemble",
    )(z, *inner, *straddle)


def plan(mesh):
    dates, rows, cols = (mesh.shape[name] for name in ("date", "row", "col"))
    high, low, core = 2, cols // 2, 2
    reach = high * low

    def place(r, c):
        x, y = r // high, (r % high) * low + c // core
        y = (y + 1) % reach
        return x * high + y // low, (y % low) * core + c % core

    def flat(r, c):
        return (r % rows) * cols + c % cols

    def spot(z, r, c):
        return (z % dates) * rows * cols + flat(r, c)

    tiles = [(r, c) for r in range(rows) for c in range(cols)]

    def route(down, right):
        return [(flat(r + down, c + right), flat(*place(r, c))) for r, c in tiles]

    def forward(kind, k):
        pairs = []
        for z in range(dates):
            q = (z + k) % dates
            right = q % 2 if kind == "straddle" else 0
            for r, c in tiles:
                pairs.append((spot(z, *place(r, c)), spot(q, r + q // 2, c + right)))
        return pairs

    def last(row, col):
        y = (row % high) * low + col // core
        y = (y + reach - 1) % reach
        r = (row // high) * high + y // low
        c = (y % low) * core + col % core
        return (r == rows - 1).astype(jnp.int32), (c == cols - 1).astype(jnp.int32)

    return {
        "low": route(0, 0),
        "high": route(1, 0),
        "low_right": route(0, 1),
        "high_right": route(1, 1),
        "inner": [forward("inner", k) for k in range(dates)],
        "straddle": [forward("straddle", k) for k in range(dates)],
        "last": last,
    }


def solution(mesh):
    placed = (P("date", "row", "col", None),) + (P(),) * 14
    return jax.shard_map(
        functools.partial(local, plan(mesh)),
        mesh=mesh,
        in_specs=placed,
        out_specs=P("date", "row", "col", None),
        check_vma=False,
    )
```

```python
import functools
import math

import jax
import jax.numpy as jnp
from jax import lax
from jax.experimental import pallas as pl
from jax.experimental.pallas import tpu as pltpu
from jax.sharding import PartitionSpec as P

WINDOW = 8
SHIFT = 4
POSITIONS = WINDOW * WINDOW
PAIR = 2 * POSITIONS
MASKED = -1000000000.0
FULL_PRECISION = lax.Precision.HIGHEST
BF16 = jnp.bfloat16
F32 = jnp.float32
MIB = 1024 * 1024

VMEM = pl.BlockSpec(memory_space=pltpu.VMEM)
SMEM = pl.BlockSpec(memory_space=pltpu.SMEM)
ANY = pl.BlockSpec(memory_space=pl.ANY)


def dot(a, b):
    return jnp.dot(a, b, preferred_element_type=F32)


def dot_first(a, b):
    return lax.dot_general(a, b, (((0,), (0,)), ((), ())), preferred_element_type=F32)


def dot_last(a, b):
    return lax.dot_general(a, b, (((1,), (1,)), ((), ())), preferred_element_type=F32)


def layer_norm(vector, gain):
    average = jnp.mean(vector, axis=-1, keepdims=True)
    centred = vector - average
    variance = jnp.mean(centred * centred, axis=-1, keepdims=True)
    return centred * lax.rsqrt(variance + 1e-05) * gain


def gelu(x):
    return 0.5 * x * (1.0 + lax.erf(x * math.sqrt(0.5)))


def column_blocks(total, width):
    return [(start, min(start + width, total)) for start in range(0, total, width)]


def project(tokens, weight, queries, keys, values):
    features = weight.shape[0]
    lead = features // 128 * 128
    edge = 2 * features
    for first, last in column_blocks(weight.shape[1], 256):
        block = dot(tokens, weight[:, first:last]).astype(BF16)
        if first < features:
            stop = min(last, features)
            queries[first:stop, :] = block.T[: stop - first]
        start, stop = max(first, lead), min(last, edge)
        if start < stop:
            keys[:, start - lead : stop - lead] = block[:, start - first : stop - first]
        if last > edge:
            start = max(first, edge)
            values[start - edge : last - edge, :] = block[:, start - first :].T


def head_blocks(heads, size, features):
    offset = features % 128
    blocks = []
    for start in range(0, heads * size + offset, 128):
        blocks.append(
            [
                (h, offset + h * size - start)
                for h in range(heads)
                if start <= offset + h * size < start + 128
            ]
        )
    return blocks


def spread_queries(queries, block, size, span):
    columns = []
    for h, start in block:
        parts = [queries[h * size : (h + 1) * size, span]]
        if start:
            parts.insert(0, jnp.zeros((start, 128), BF16))
        if start + size < 128:
            parts.append(jnp.zeros((128 - size - start, 128), BF16))
        columns.append(jnp.concatenate(parts, axis=0))
    return jnp.concatenate(columns, axis=1)


def staggered(units, early, late):
    ready = early(units[0])
    for i, unit in enumerate(units):
        held = ready
        if i + 1 < len(units):
            ready = early(units[i + 1])
        late(unit, held)


def pack(pixels, low, high, low_right, high_right, work):
    dates, rows, cols, features = pixels.shape
    half = rows // 2
    for d in range(dates):
        work[...] = pixels[d].astype(F32)
        for first, out, right in ((half, low, low_right), (0, high, high_right)):
            lines = range(first, first + half)
            inner = [work[i, SHIFT : SHIFT + WINDOW, :] for i in lines]
            outer = [work[i, cols - SHIFT : cols, :] for i in lines]
            out[d] = jnp.concatenate(inner + outer, axis=0).astype(BF16)
            right[d] = jnp.concatenate([work[i, :SHIFT, :] for i in lines], axis=0).astype(BF16)


def bias_kernel(first, second, _, out, table):
    units = first.shape[1]
    heads = second.shape[0]
    layer = jnp.concatenate([first[...], jnp.zeros((6, units), F32)], axis=0).T
    lane = lax.broadcasted_iota(jnp.int32, (1, 128), 1)

    def mapped(offset):
        distance = offset.astype(F32) * (8.0 / (WINDOW - 1))
        size = jnp.log(jnp.abs(distance) + 1.0) * (1.0 / (3.0 * math.log(2.0)))
        return jnp.where(distance < 0, -size, size)

    row_part = layer[:, 0:1] * mapped(lax.shift_right_logical(lane, 3) - (WINDOW - 1))
    col_weight = jnp.broadcast_to(layer[:, 1:2], (units, 128))
    for col in range(WINDOW):
        hidden = jnp.maximum(row_part + col_weight * mapped((lane & 7) - col), 0.0)
        logits = jnp.dot(second[...], hidden, precision=FULL_PRECISION, preferred_element_type=F32)
        table[col * 32 : col * 32 + heads, :] = 16.0 / (1.0 + jnp.exp(-logits))
    wide = lax.broadcasted_iota(jnp.int32, (WINDOW, 128), 1)
    for h in range(heads):
        lines = table[pl.ds(h, WINDOW, stride=32), :]
        for row in range(WINDOW):
            start = (WINDOW - 1 - row) * WINDOW
            left = pltpu.roll(lines, (128 - start) % 128, 1)
            right = pltpu.roll(lines, POSITIONS - start, 1)
            out[h, row * WINDOW : (row + 1) * WINDOW, :] = jnp.where(wide < POSITIONS, left, right)


def inner_tokens(low, high):
    inner = WINDOW // 2 * WINDOW
    tokens = jnp.concatenate([low[:, :inner], high[:, :inner]], axis=1)
    return tokens.reshape(tokens.shape[0] * POSITIONS, tokens.shape[2])


def straddle_tokens(low_left, high_left, low_right, high_right, work):
    half = WINDOW // 2
    for side, (left, right) in enumerate(((low_left, low_right), (high_left, high_right))):
        for d in range(left.shape[0]):
            left_rows = left[d, half * WINDOW :, :].astype(F32)
            right_rows = right[d].astype(F32)
            for i in range(half):
                base = d * POSITIONS + (side * half + i) * WINDOW
                part = slice(i * SHIFT, (i + 1) * SHIFT)
                work[base : base + SHIFT, :] = left_rows[part, :]
                work[base + SHIFT : base + WINDOW, :] = right_rows[part, :]
    return work[...].astype(BF16)


def attend(tokens, last_row, last_col, scale, bias, qkv, mixed_heads, scratch):
    queries, keys, low_keys, values = scratch
    features = qkv.shape[0]
    heads = bias.shape[0]
    size = features // heads
    token_total = tokens.shape[0]
    project(tokens, qkv, queries, keys, values)

    wide_keys = keys[...].astype(F32)
    column = lax.broadcasted_iota(jnp.int32, (wide_keys.shape[1], 128), 0) - features % 128
    owner = lax.broadcasted_iota(jnp.int32, (wide_keys.shape[1], 128), 1)
    member = jnp.where((column >= owner * size) & (column < (owner + 1) * size), 1.0, 0.0)
    member = member.astype(BF16)

    def halves(x):
        top = x.astype(BF16)
        return top, (x - top.astype(F32)).astype(BF16)

    squares, rest = halves(wide_keys * wide_keys)
    norms = dot(squares, member) + dot(rest, member)
    shrink, rest = halves(lax.rsqrt(jnp.maximum(norms, 1.0)))
    shrink = dot_last(shrink, member) + dot_last(rest, member)
    keys[...], low_keys[...] = halves(wide_keys * shrink)

    lane = lax.broadcasted_iota(jnp.int32, (POSITIONS, PAIR), 1)
    line = lax.broadcasted_iota(jnp.int32, (POSITIONS, PAIR), 0)
    first_window = lane < POSITIONS
    apart = (((lane ^ line) & 32) != 0) & (last_row[0] != 0)
    if last_col is not None:
        apart = apart | ((((lane ^ line) & 4) != 0) & (last_col[0] != 0))
    closed = jnp.where(apart, MASKED, 0.0)
    keep_first = jnp.where(first_window, 1.0, 0.0).astype(BF16)
    keep_second = jnp.where(first_window, 0.0, 1.0).astype(BF16)
    blocks = head_blocks(heads, size, features)

    def early(unit):
        b, p = unit
        span = slice(p * PAIR, (p + 1) * PAIR)
        columns = slice(b * 128, (b + 1) * 128)
        left = jnp.concatenate([keys[span, columns], low_keys[span, columns]], axis=1)
        right = spread_queries(queries, blocks[b], size, span)
        return dot(left, jnp.concatenate([right, right], axis=0))

    def late(unit, both):
        b, p = unit
        span = slice(p * PAIR, (p + 1) * PAIR)
        held = []
        for i, (h, _) in enumerate(blocks[b]):
            query = queries[h * size : (h + 1) * size, span].astype(F32)
            factor = scale[h] * lax.rsqrt(
                jnp.maximum(jnp.sum(query * query, axis=0, keepdims=True), 1.0)
            )
            mine = both[:, i * PAIR : (i + 1) * PAIR]
            scores = jnp.where(first_window, mine[:POSITIONS], mine[POSITIONS:])
            scores = scores * factor + (bias[h] + closed)
            weight = jnp.exp(scores - jnp.max(scores, axis=0, keepdims=True))
            total = jnp.sum(weight, axis=0, keepdims=True)
            narrow = weight.astype(BF16)
            spread = jnp.concatenate([narrow * keep_first, narrow * keep_second], axis=0)
            held.append((h, spread, 1.0 / total))
        for h, spread, inverse in held:
            result = dot(values[h * size : (h + 1) * size, span], spread) * inverse
            mixed_heads[h * size : (h + 1) * size, span] = result.astype(BF16)

    units = [(b, p) for b in range(len(blocks)) for p in range(token_total // PAIR)]
    staggered(units, early, late)

def settle(tokens, mixed_heads, lift, up, down, attention_gain, forward_gain):
    features = tokens.shape[1]
    projected = dot_first(mixed_heads[...], lift[...])
    gain = attention_gain[...].reshape(1, features)
    resid = (tokens.astype(F32) + layer_norm(projected, gain)).astype(BF16)

    parts = []

    def raise_block(span):
        return dot(resid, up[:, slice(*span)])

    def lower_block(span, raised):
        parts.append(dot_last(gelu(raised).astype(BF16), down[:, slice(*span)]))
        if len(parts) > 1:
            parts[:] = [parts[0] + parts[1]]

    staggered(column_blocks(up.shape[1], 512), raise_block, lower_block)
    (lowered,) = parts
    return resid.astype(F32) + layer_norm(lowered, forward_gain[...].reshape(1, features))


def send_quarters(quarters, place, outs):
    for q, quarter in enumerate(quarters):
        for k in range(4):

            @pl.when((place[0] + k) % 4 == q)
            def _(quarter=quarter, k=k):
                outs[k][...] = quarter


def inner_attention(low, high, last_row, scale, bias, qkv, mixed_heads, *scratch):
    attend(inner_tokens(low, high), last_row, None, scale, bias, qkv, mixed_heads, scratch)


def inner_settle(place, low, high, mixed_heads, lift, up, down, gain, forward_gain, *outs):
    *outs, token = outs
    token[...] = jnp.zeros(token.shape, F32)
    tokens = inner_tokens(low, high)
    mixed = settle(tokens, mixed_heads, lift, up, down, gain, forward_gain)
    narrow = mixed.astype(BF16).reshape(low.shape[0], 4, POSITIONS // 4, low.shape[2])
    send_quarters([narrow[:, q] for q in range(4)], place, outs)


def straddle_window(place, last_row, last_col, scale, *refs):
    corners, _, bias, qkv, *refs = refs[:4], *refs[4:]
    lift, up, down, attention_gain, forward_gain, *refs = refs
    outs, token, scratch, mixed_heads, work = refs[:4], refs[4], refs[5:9], refs[9], refs[10]
    token[...] = jnp.zeros(token.shape, F32)
    tokens = straddle_tokens(*corners, work)
    attend(tokens, last_row, last_col, scale, bias, qkv, mixed_heads, scratch)
    work[...] = settle(tokens, mixed_heads, lift, up, down, attention_gain, forward_gain)
    half = WINDOW // 2
    quarters = []
    for q in range(4):
        quarter = []
        for d in range(corners[0].shape[0]):
            lines = []
            for i in range(half):
                base = d * POSITIONS + ((q // 2) * half + i) * WINDOW + (q % 2) * SHIFT
                lines.append(work[base : base + SHIFT, :])
            quarter.append(jnp.concatenate(lines, axis=0).astype(BF16)[None])
        quarters.append(jnp.concatenate(quarter, axis=0))
    send_quarters(quarters, place, outs)


def time_kernel(size, place, rank, *refs):
    pieces, refs = refs[:4], refs[4:]
    _, embedding, time_gain, qkv, lift, *refs = refs
    outs, token, refs = refs[:4], refs[4], refs[5:]
    queries, keys, values, mixed_heads = refs
    features = qkv.shape[0]
    heads = features // size
    z = place[0]
    own, pixel_count, _ = pieces[0].shape
    dates = 4 * own
    group = 128 // dates
    groups = pixel_count // group
    token[...] = jnp.zeros(token.shape, F32)

    gain = time_gain[...].reshape(1, 1, features)
    wide = []
    normed = []
    for k in range(4):
        block = pieces[k][...].astype(F32)
        source = (z + 4 - k) % 4
        lines = layer_norm(block, gain)
        for i in range(own):
            line = embedding[pl.ds(rank[source * own + i], 1), :]
            normed.append((lines[i] + line)[None])
        wide.append(block)
    normed = jnp.concatenate(normed, axis=0)
    tokens = jnp.concatenate(
        [
            normed[:, g * group : (g + 1) * group, :].reshape(128, features).astype(BF16)
            for g in range(groups)
        ],
        axis=0,
    )
    project(tokens, qkv, queries, keys, values)

    lane = lax.broadcasted_iota(jnp.int32, (group, 128), 1)
    line = lax.broadcasted_iota(jnp.int32, (group, 128), 0)
    same = jnp.where((lane & (group - 1)) == line, 1.0, 0.0)
    shrink = size ** (-0.5)
    blocks = head_blocks(heads, size, features)

    def early(unit):
        b, g = unit
        span = slice(g * 128, (g + 1) * 128)
        right = spread_queries(queries, blocks[b], size, span)
        return dot(keys[span, b * 128 : (b + 1) * 128], right)

    def late(unit, both):
        b, g = unit
        span = slice(g * 128, (g + 1) * 128)
        held = []
        for i, (h, _) in enumerate(blocks[b]):
            scores = both[:, i * 128 : (i + 1) * 128].reshape(dates, group, 128)
            weight = jnp.exp((scores - jnp.max(scores, axis=0, keepdims=True)) * shrink)
            inverse = same / jnp.sum(weight, axis=0)
            held.append((h, (weight * inverse[None]).reshape(128, 128).astype(BF16)))
        for h, probs in held:
            result = dot(values[h * size : (h + 1) * size, span], probs)
            mixed_heads[h * size : (h + 1) * size, span] = result.astype(BF16)

    units = [(b, g) for b in range(len(blocks)) for g in range(groups)]
    staggered(units, early, late)

    lifted = dot_first(mixed_heads[...], lift[...])
    for k in range(4):
        parts = [
            lifted[g * 128 : (g + 1) * 128].reshape(dates, group, features)[k * own : (k + 1) * own]
            for g in range(groups)
        ]
        outs[k][...] = (wide[k] + jnp.concatenate(parts, axis=1)).astype(BF16)


def assemble(place, *refs):
    inner, straddle, (out, work) = refs[:4], refs[4:8], refs[8:]
    dates, rows, cols, features = out.shape
    half = rows // 2
    z = place[0]
    for k in range(4):
        q = (z + k) % 4
        block = inner[k][...].astype(F32)
        top = (2 * q + half) % rows
        for d in range(dates):
            for j in range(2):
                work[d, top + j, SHIFT : SHIFT + WINDOW, :] = block[d, j * WINDOW : (j + 1) * WINDOW]
    for parity in range(2):

        @pl.when(z % 2 == parity)
        def _(parity=parity):
            for k in range(4):
                q = (z + k) % 4
                block = straddle[k][...].astype(F32)
                top = jnp.where(q < 2, half, 0)
                left = cols - SHIFT if (parity + k) % 2 == 0 else 0
                for d in range(dates):
                    for i in range(half):
                        work[d, top + i, left : left + SHIFT, :] = block[
                            d, i * SHIFT : (i + 1) * SHIFT
                        ]

    out[...] = work[...].astype(BF16)


def call(kernel, out_shape, in_specs, scratch, flops, moved, name, room=8):
    return pl.pallas_call(
        kernel,
        out_shape=out_shape,
        in_specs=in_specs,
        out_specs=jax.tree.map(lambda _: VMEM, out_shape),
        scratch_shapes=scratch,
        compiler_params=pltpu.CompilerParams(vmem_limit_bytes=room * MIB),
        cost_estimate=pl.CostEstimate(flops=flops, bytes_accessed=moved, transcendentals=0),
        name=name,
    )


def local(
    routes,
    pixels,
    window_query_key_value_weight,
    head_logit_scale,
    bias_network_first,
    bias_network_second,
    window_output_weight,
    attention_norm_gain,
    feedforward_up_weight,
    feedforward_down_weight,
    feedforward_norm_gain,
    temporal_norm_gain,
    date_rank_embedding,
    acquisition_rank,
    temporal_query_key_value_weight,
    temporal_output_weight,
):
    dates, rows, cols, features = pixels.shape
    heads = head_logit_scale.shape[0]
    hidden = feedforward_up_weight.shape[1]
    plane = ("row", "col")
    space = ("date", "row", "col")
    token_total = dates * POSITIONS
    part = POSITIONS // 4
    date_axis = lax.axis_size("date")
    z = lax.axis_index("date")
    last_row, last_col = routes["last"](lax.axis_index("row"), lax.axis_index("col"))
    z = z.astype(jnp.int32).reshape(1)
    last_row, last_col = last_row.reshape(1), last_col.reshape(1)

    piece_shape = jax.ShapeDtypeStruct((dates, POSITIONS // 2 + part, features), BF16)
    part_shape = jax.ShapeDtypeStruct((dates, part, features), BF16)
    token_shape = jax.ShapeDtypeStruct((8, 128), F32)
    key_columns = -(-(features % 128 + features) // 128) * 128
    tile_bytes = pixels.size * 2

    packed = call(
        pack,
        [piece_shape] * 2 + [part_shape] * 2,
        [VMEM],
        [pltpu.VMEM(pixels.shape[1:], F32)],
        10**10,
        tile_bytes * 2,
        "pack",
        4,
    )(pixels)
    low, high, low_right, high_right = (
        lax.ppermute(piece, plane, routes[name])
        for piece, name in zip(packed, ("low", "high", "low_right", "high_right"))
    )
    bias = call(
        bias_kernel,
        jax.ShapeDtypeStruct((heads, POSITIONS, PAIR), F32),
        [VMEM] * 3,
        [pltpu.VMEM((WINDOW * 32, 128), F32)],
        10**9,
        10**6,
        "position_bias",
        6,
    )(bias_network_first, bias_network_second.T, window_query_key_value_weight)

    projected = [
        pltpu.VMEM((features, token_total), BF16),
        pltpu.VMEM((token_total, key_columns), BF16),
        pltpu.VMEM((token_total, key_columns), BF16),
        pltpu.VMEM((features, token_total), BF16),
        pltpu.VMEM((features, token_total), BF16),
    ]

    weights = (
        window_output_weight,
        feedforward_up_weight,
        feedforward_down_weight.T,
        attention_norm_gain,
        feedforward_norm_gain,
    )
    settle_flops = 2 * token_total * features * (features + 2 * hidden)
    attend_flops = 2 * token_total * features * 3 * features * 2

    def inner_layer(low, high):
        mixed_heads = call(
            inner_attention,
            jax.ShapeDtypeStruct((features, token_total), BF16),
            [VMEM] * 2 + [SMEM] * 2 + [VMEM] * 2,
            projected[:4],
            attend_flops,
            4 * 10**6,
            "inner_attention",
            14,
        )(low, high, last_row, head_logit_scale, bias, window_query_key_value_weight)
        return call(
            inner_settle,
            [part_shape] * 4 + [token_shape],
            [SMEM] + [VMEM] * 8,
            [],
            settle_flops,
            9 * 10**6,
            "inner_settle",
            20,
        )(z, low, high, mixed_heads, *weights)

    def straddle_layer(corners, token):
        return call(
            straddle_window,
            [part_shape] * 4 + [token_shape],
            [SMEM] * 4 + [VMEM] * 4 + [ANY] + [VMEM] * 7,
            projected + [pltpu.VMEM((token_total, features), F32)],
            attend_flops + settle_flops,
            13 * 10**6,
            "straddle_window",
            24,
        )(
            z,
            last_row,
            last_col,
            head_logit_scale,
            *corners,
            token,
            bias,
            window_query_key_value_weight,
            *weights,
        )

    def time_layer(pieces, token):
        return call(
            functools.partial(time_kernel, features // heads),
            [part_shape] * 4 + [token_shape],
            [SMEM, SMEM] + [VMEM] * 4 + [ANY] + [VMEM] * 4,
            projected[:2] + projected[3:],
            2 * token_total * features * 4 * features,
            5 * 10**6,
            "time_layer",
            14,
        )(
            z,
            acquisition_rank,
            *pieces,
            token,
            date_rank_embedding,
            temporal_norm_gain,
            temporal_query_key_value_weight,
            temporal_output_weight,
        )

    def to_dates(pieces, kind):
        return [lax.ppermute(piece, space, routes[kind][k]) for k, piece in enumerate(pieces)]

    def to_home(pieces):
        return [
            piece
            if k == 0
            else lax.ppermute(piece, "date", [(i, (i - k) % date_axis) for i in range(date_axis)])
            for k, piece in enumerate(pieces)
        ]

    *inner, token = inner_layer(low, high)
    inner = to_dates(inner, "inner")
    *straddle, token = straddle_layer([low, high, low_right, high_right], token)
    straddle = to_dates(straddle, "straddle")
    *inner, token = time_layer(inner, token)
    inner = to_home(inner)
    *straddle, token = time_layer(straddle, token)
    straddle = to_home(straddle)
    return call(
        assemble,
        jax.ShapeDtypeStruct(pixels.shape, BF16),
        [SMEM] + [VMEM] * 8,
        [pltpu.VMEM(pixels.shape, F32)],
        0,
        tile_bytes * 2,
        "assemble",
    )(z, *inner, *straddle)


def plan(mesh):
    dates, rows, cols = (mesh.shape[name] for name in ("date", "row", "col"))
    high, low, core = 2, cols // 2, 2
    reach = high * low

    def place(r, c):
        x, y = r // high, (r % high) * low + c // core
        y = (y + 1) % reach
        return x * high + y // low, (y % low) * core + c % core

    def flat(r, c):
        return (r % rows) * cols + c % cols

    def spot(z, r, c):
        return (z % dates) * rows * cols + flat(r, c)

    tiles = [(r, c) for r in range(rows) for c in range(cols)]

    def route(down, right):
        return [(flat(r + down, c + right), flat(*place(r, c))) for r, c in tiles]

    def forward(kind, k):
        pairs = []
        for z in range(dates):
            q = (z + k) % dates
            right = q % 2 if kind == "straddle" else 0
            for r, c in tiles:
                pairs.append((spot(z, *place(r, c)), spot(q, r + q // 2, c + right)))
        return pairs

    def last(row, col):
        y = (row % high) * low + col // core
        y = (y + reach - 1) % reach
        r = (row // high) * high + y // low
        c = (y % low) * core + col % core
        return (r == rows - 1).astype(jnp.int32), (c == cols - 1).astype(jnp.int32)

    return {
        "low": route(0, 0),
        "high": route(1, 0),
        "low_right": route(0, 1),
        "high_right": route(1, 1),
        "inner": [forward("inner", k) for k in range(dates)],
        "straddle": [forward("straddle", k) for k in range(dates)],
        "last": last,
    }


def solution(mesh):
    placed = (P("date", "row", "col", None),) + (P(),) * 14
    return jax.shard_map(
        functools.partial(local, plan(mesh)),
        mesh=mesh,
        in_specs=placed,
        out_specs=P("date", "row", "col", None),
        check_vma=False,
    )
```

```python
import functools
import math

import jax
import jax.numpy as jnp
from jax import lax
from jax.experimental import pallas as pl
from jax.experimental.pallas import tpu as pltpu
from jax.sharding import PartitionSpec as P

WINDOW = 8
SHIFT = 4
POSITIONS = WINDOW * WINDOW
PAIR = 2 * POSITIONS
MASKED = -1000000000.0
FULL_PRECISION = lax.Precision.HIGHEST
BF16 = jnp.bfloat16
F32 = jnp.float32
MIB = 1024 * 1024

VMEM = pl.BlockSpec(memory_space=pltpu.VMEM)
SMEM = pl.BlockSpec(memory_space=pltpu.SMEM)
ANY = pl.BlockSpec(memory_space=pl.ANY)


def dot(a, b):
    return jnp.dot(a, b, preferred_element_type=F32)


def dot_first(a, b):
    return lax.dot_general(a, b, (((0,), (0,)), ((), ())), preferred_element_type=F32)


def dot_last(a, b):
    return lax.dot_general(a, b, (((1,), (1,)), ((), ())), preferred_element_type=F32)


def layer_norm(vector, gain):
    average = jnp.mean(vector, axis=-1, keepdims=True)
    centred = vector - average
    variance = jnp.mean(centred * centred, axis=-1, keepdims=True)
    return centred * lax.rsqrt(variance + 1e-05) * gain


def gelu(x):
    return 0.5 * x * (1.0 + lax.erf(x * math.sqrt(0.5)))


def column_blocks(total, width):
    return [(start, min(start + width, total)) for start in range(0, total, width)]


def project(tokens, weight, queries, keys, values):
    features = weight.shape[0]
    lead = features // 128 * 128
    edge = 2 * features
    for first, last in column_blocks(weight.shape[1], 256):
        block = dot(tokens, weight[:, first:last]).astype(BF16)
        if first < features:
            stop = min(last, features)
            queries[first:stop, :] = block.T[: stop - first]
        start, stop = max(first, lead), min(last, edge)
        if start < stop:
            keys[:, start - lead : stop - lead] = block[:, start - first : stop - first]
        if last > edge:
            start = max(first, edge)
            values[start - edge : last - edge, :] = block[:, start - first :].T


def head_blocks(heads, size, features):
    offset = features % 128
    blocks = []
    for start in range(0, heads * size + offset, 128):
        blocks.append(
            [
                (h, offset + h * size - start)
                for h in range(heads)
                if start <= offset + h * size < start + 128
            ]
        )
    return blocks


def spread_queries(queries, block, size, span):
    columns = []
    for h, start in block:
        parts = [queries[h * size : (h + 1) * size, span]]
        if start:
            parts.insert(0, jnp.zeros((start, 128), BF16))
        if start + size < 128:
            parts.append(jnp.zeros((128 - size - start, 128), BF16))
        columns.append(jnp.concatenate(parts, axis=0))
    return jnp.concatenate(columns, axis=1)


def staggered(units, early, late):
    ready = early(units[0])
    for i, unit in enumerate(units):
        held = ready
        if i + 1 < len(units):
            ready = early(units[i + 1])
        late(unit, held)


def pack(pixels, low, high, low_right, high_right, work):
    dates, rows, cols, features = pixels.shape
    half = rows // 2
    for d in range(dates):
        work[...] = pixels[d].astype(F32)
        for first, out, right in ((half, low, low_right), (0, high, high_right)):
            lines = range(first, first + half)
            inner = [work[i, SHIFT : SHIFT + WINDOW, :] for i in lines]
            outer = [work[i, cols - SHIFT : cols, :] for i in lines]
            out[d] = jnp.concatenate(inner + outer, axis=0).astype(BF16)
            right[d] = jnp.concatenate([work[i, :SHIFT, :] for i in lines], axis=0).astype(BF16)


def bias_kernel(first, second, out, table):
    units = first.shape[1]
    heads = second.shape[0]
    layer = jnp.concatenate([first[...], jnp.zeros((6, units), F32)], axis=0).T
    lane = lax.broadcasted_iota(jnp.int32, (1, 128), 1)

    def mapped(offset):
        distance = offset.astype(F32) * (8.0 / (WINDOW - 1))
        size = jnp.log(jnp.abs(distance) + 1.0) * (1.0 / (3.0 * math.log(2.0)))
        return jnp.where(distance < 0, -size, size)

    row_part = layer[:, 0:1] * mapped(lax.shift_right_logical(lane, 3) - (WINDOW - 1))
    col_weight = jnp.broadcast_to(layer[:, 1:2], (units, 128))
    for col in range(WINDOW):
        hidden = jnp.maximum(row_part + col_weight * mapped((lane & 7) - col), 0.0)
        logits = jnp.dot(second[...], hidden, precision=FULL_PRECISION, preferred_element_type=F32)
        table[col * 32 : col * 32 + heads, :] = 16.0 / (1.0 + jnp.exp(-logits))
    wide = lax.broadcasted_iota(jnp.int32, (WINDOW, 128), 1)
    for h in range(heads):
        lines = table[pl.ds(h, WINDOW, stride=32), :]
        for row in range(WINDOW):
            start = (WINDOW - 1 - row) * WINDOW
            left = pltpu.roll(lines, (128 - start) % 128, 1)
            right = pltpu.roll(lines, POSITIONS - start, 1)
            out[h, row * WINDOW : (row + 1) * WINDOW, :] = jnp.where(wide < POSITIONS, left, right)


def inner_tokens(low, high):
    inner = WINDOW // 2 * WINDOW
    tokens = jnp.concatenate([low[:, :inner], high[:, :inner]], axis=1)
    return tokens.reshape(tokens.shape[0] * POSITIONS, tokens.shape[2])


def straddle_tokens(low_left, high_left, low_right, high_right, work):
    half = WINDOW // 2
    for side, (left, right) in enumerate(((low_left, low_right), (high_left, high_right))):
        for d in range(left.shape[0]):
            left_rows = left[d, half * WINDOW :, :].astype(F32)
            right_rows = right[d].astype(F32)
            for i in range(half):
                base = d * POSITIONS + (side * half + i) * WINDOW
                part = slice(i * SHIFT, (i + 1) * SHIFT)
                work[base : base + SHIFT, :] = left_rows[part, :]
                work[base + SHIFT : base + WINDOW, :] = right_rows[part, :]
    return work[...].astype(BF16)


def attend(tokens, last_row, last_col, scale, bias, qkv, mixed_heads, scratch):
    queries, keys, low_keys, values = scratch
    features = qkv.shape[0]
    heads = bias.shape[0]
    size = features // heads
    token_total = tokens.shape[0]
    project(tokens, qkv, queries, keys, values)

    wide_keys = keys[...].astype(F32)
    column = lax.broadcasted_iota(jnp.int32, (wide_keys.shape[1], 128), 0) - features % 128
    owner = lax.broadcasted_iota(jnp.int32, (wide_keys.shape[1], 128), 1)
    member = jnp.where((column >= owner * size) & (column < (owner + 1) * size), 1.0, 0.0)
    member = member.astype(BF16)

    def halves(x):
        top = x.astype(BF16)
        return top, (x - top.astype(F32)).astype(BF16)

    squares, rest = halves(wide_keys * wide_keys)
    norms = dot(squares, member) + dot(rest, member)
    shrink, rest = halves(lax.rsqrt(jnp.maximum(norms, 1.0)))
    shrink = dot_last(shrink, member) + dot_last(rest, member)
    keys[...], low_keys[...] = halves(wide_keys * shrink)

    lane = lax.broadcasted_iota(jnp.int32, (POSITIONS, PAIR), 1)
    line = lax.broadcasted_iota(jnp.int32, (POSITIONS, PAIR), 0)
    first_window = lane < POSITIONS
    apart = (((lane ^ line) & 32) != 0) & (last_row[0] != 0)
    if last_col is not None:
        apart = apart | ((((lane ^ line) & 4) != 0) & (last_col[0] != 0))
    closed = jnp.where(apart, MASKED, 0.0)
    keep_first = jnp.where(first_window, 1.0, 0.0).astype(BF16)
    keep_second = jnp.where(first_window, 0.0, 1.0).astype(BF16)
    blocks = head_blocks(heads, size, features)

    def early(unit):
        b, p = unit
        span = slice(p * PAIR, (p + 1) * PAIR)
        columns = slice(b * 128, (b + 1) * 128)
        left = jnp.concatenate([keys[span, columns], low_keys[span, columns]], axis=1)
        right = spread_queries(queries, blocks[b], size, span)
        return dot(left, jnp.concatenate([right, right], axis=0))

    def late(unit, both):
        b, p = unit
        span = slice(p * PAIR, (p + 1) * PAIR)
        held = []
        for i, (h, _) in enumerate(blocks[b]):
            query = queries[h * size : (h + 1) * size, span].astype(F32)
            factor = scale[h] * lax.rsqrt(
                jnp.maximum(jnp.sum(query * query, axis=0, keepdims=True), 1.0)
            )
            mine = both[:, i * PAIR : (i + 1) * PAIR]
            scores = jnp.where(first_window, mine[:POSITIONS], mine[POSITIONS:])
            scores = scores * factor + (bias[h] + closed)
            weight = jnp.exp(scores - jnp.max(scores, axis=0, keepdims=True))
            total = jnp.sum(weight, axis=0, keepdims=True)
            narrow = weight.astype(BF16)
            spread = jnp.concatenate([narrow * keep_first, narrow * keep_second], axis=0)
            held.append((h, spread, 1.0 / total))
        for h, spread, inverse in held:
            result = dot(values[h * size : (h + 1) * size, span], spread) * inverse
            mixed_heads[h * size : (h + 1) * size, span] = result.astype(BF16)

    units = [(b, p) for b in range(len(blocks)) for p in range(token_total // PAIR)]
    staggered(units, early, late)

def settle(tokens, mixed_heads, lift, up, down, attention_gain, forward_gain):
    features = tokens.shape[1]
    projected = dot_first(mixed_heads[...], lift[...])
    gain = attention_gain[...].reshape(1, features)
    resid = (tokens.astype(F32) + layer_norm(projected, gain)).astype(BF16)

    parts = []

    def raise_block(span):
        return dot(resid, up[:, slice(*span)])

    def lower_block(span, raised):
        parts.append(dot_last(gelu(raised).astype(BF16), down[:, slice(*span)]))
        if len(parts) > 1:
            parts[:] = [parts[0] + parts[1]]

    staggered(column_blocks(up.shape[1], 512), raise_block, lower_block)
    (lowered,) = parts
    return resid.astype(F32) + layer_norm(lowered, forward_gain[...].reshape(1, features))


def send_quarters(quarters, place, outs):
    for q, quarter in enumerate(quarters):
        for k in range(4):

            @pl.when((place[0] + k) % 4 == q)
            def _(quarter=quarter, k=k):
                outs[k][...] = quarter


def inner_attention(low, high, last_row, scale, bias, qkv, mixed_heads, *scratch):
    attend(inner_tokens(low, high), last_row, None, scale, bias, qkv, mixed_heads, scratch)


def inner_settle(place, low, high, mixed_heads, lift, up, down, gain, forward_gain, *outs):
    *outs, token = outs
    token[...] = jnp.zeros(token.shape, F32)
    tokens = inner_tokens(low, high)
    mixed = settle(tokens, mixed_heads, lift, up, down, gain, forward_gain)
    narrow = mixed.astype(BF16).reshape(low.shape[0], 4, POSITIONS // 4, low.shape[2])
    send_quarters([narrow[:, q] for q in range(4)], place, outs)


def straddle_window(place, last_row, last_col, scale, *refs):
    corners, _, bias, qkv, *refs = refs[:4], *refs[4:]
    lift, up, down, attention_gain, forward_gain, *refs = refs
    outs, token, scratch, mixed_heads, work = refs[:4], refs[4], refs[5:9], refs[9], refs[10]
    token[...] = jnp.zeros(token.shape, F32)
    tokens = straddle_tokens(*corners, work)
    attend(tokens, last_row, last_col, scale, bias, qkv, mixed_heads, scratch)
    work[...] = settle(tokens, mixed_heads, lift, up, down, attention_gain, forward_gain)
    half = WINDOW // 2
    quarters = []
    for q in range(4):
        quarter = []
        for d in range(corners[0].shape[0]):
            lines = []
            for i in range(half):
                base = d * POSITIONS + ((q // 2) * half + i) * WINDOW + (q % 2) * SHIFT
                lines.append(work[base : base + SHIFT, :])
            quarter.append(jnp.concatenate(lines, axis=0).astype(BF16)[None])
        quarters.append(jnp.concatenate(quarter, axis=0))
    send_quarters(quarters, place, outs)


def time_kernel(size, place, rank, *refs):
    pieces, refs = refs[:4], refs[4:]
    _, embedding, time_gain, qkv, lift, *refs = refs
    outs, token, refs = refs[:4], refs[4], refs[5:]
    queries, keys, values, mixed_heads = refs
    features = qkv.shape[0]
    heads = features // size
    z = place[0]
    own, pixel_count, _ = pieces[0].shape
    dates = 4 * own
    group = 128 // dates
    groups = pixel_count // group
    token[...] = jnp.zeros(token.shape, F32)

    gain = time_gain[...].reshape(1, 1, features)
    wide = []
    normed = []
    for k in range(4):
        block = pieces[k][...].astype(F32)
        source = (z + 4 - k) % 4
        lines = layer_norm(block, gain)
        for i in range(own):
            line = embedding[pl.ds(rank[source * own + i], 1), :]
            normed.append((lines[i] + line)[None])
        wide.append(block)
    normed = jnp.concatenate(normed, axis=0)
    tokens = jnp.concatenate(
        [
            normed[:, g * group : (g + 1) * group, :].reshape(128, features).astype(BF16)
            for g in range(groups)
        ],
        axis=0,
    )
    project(tokens, qkv, queries, keys, values)

    lane = lax.broadcasted_iota(jnp.int32, (group, 128), 1)
    line = lax.broadcasted_iota(jnp.int32, (group, 128), 0)
    same = jnp.where((lane & (group - 1)) == line, 1.0, 0.0)
    shrink = size ** (-0.5)
    blocks = head_blocks(heads, size, features)

    def early(unit):
        b, g = unit
        span = slice(g * 128, (g + 1) * 128)
        right = spread_queries(queries, blocks[b], size, span)
        return dot(keys[span, b * 128 : (b + 1) * 128], right)

    def late(unit, both):
        b, g = unit
        span = slice(g * 128, (g + 1) * 128)
        held = []
        for i, (h, _) in enumerate(blocks[b]):
            scores = both[:, i * 128 : (i + 1) * 128].reshape(dates, group, 128)
            weight = jnp.exp((scores - jnp.max(scores, axis=0, keepdims=True)) * shrink)
            inverse = same / jnp.sum(weight, axis=0)
            held.append((h, (weight * inverse[None]).reshape(128, 128).astype(BF16)))
        for h, probs in held:
            result = dot(values[h * size : (h + 1) * size, span], probs)
            mixed_heads[h * size : (h + 1) * size, span] = result.astype(BF16)

    units = [(b, g) for b in range(len(blocks)) for g in range(groups)]
    staggered(units, early, late)

    lifted = dot_first(mixed_heads[...], lift[...])
    for k in range(4):
        parts = [
            lifted[g * 128 : (g + 1) * 128].reshape(dates, group, features)[k * own : (k + 1) * own]
            for g in range(groups)
        ]
        outs[k][...] = (wide[k] + jnp.concatenate(parts, axis=1)).astype(BF16)


def assemble(place, *refs):
    inner, straddle, (out, work) = refs[:4], refs[4:8], refs[8:]
    dates, rows, cols, features = out.shape
    half = rows // 2
    z = place[0]
    for k in range(4):
        q = (z + k) % 4
        block = inner[k][...].astype(F32)
        top = (2 * q + half) % rows
        for d in range(dates):
            for j in range(2):
                work[d, top + j, SHIFT : SHIFT + WINDOW, :] = block[d, j * WINDOW : (j + 1) * WINDOW]
    for parity in range(2):

        @pl.when(z % 2 == parity)
        def _(parity=parity):
            for k in range(4):
                q = (z + k) % 4
                block = straddle[k][...].astype(F32)
                top = jnp.where(q < 2, half, 0)
                left = cols - SHIFT if (parity + k) % 2 == 0 else 0
                for d in range(dates):
                    for i in range(half):
                        work[d, top + i, left : left + SHIFT, :] = block[
                            d, i * SHIFT : (i + 1) * SHIFT
                        ]

    out[...] = work[...].astype(BF16)


def call(kernel, out_shape, in_specs, scratch, flops, moved, name, room=8):
    return pl.pallas_call(
        kernel,
        out_shape=out_shape,
        in_specs=in_specs,
        out_specs=jax.tree.map(lambda _: VMEM, out_shape),
        scratch_shapes=scratch,
        compiler_params=pltpu.CompilerParams(vmem_limit_bytes=room * MIB),
        cost_estimate=pl.CostEstimate(flops=flops, bytes_accessed=moved, transcendentals=0),
        name=name,
    )


def local(
    routes,
    pixels,
    window_query_key_value_weight,
    head_logit_scale,
    bias_network_first,
    bias_network_second,
    window_output_weight,
    attention_norm_gain,
    feedforward_up_weight,
    feedforward_down_weight,
    feedforward_norm_gain,
    temporal_norm_gain,
    date_rank_embedding,
    acquisition_rank,
    temporal_query_key_value_weight,
    temporal_output_weight,
):
    dates, rows, cols, features = pixels.shape
    heads = head_logit_scale.shape[0]
    hidden = feedforward_up_weight.shape[1]
    plane = ("row", "col")
    space = ("date", "row", "col")
    token_total = dates * POSITIONS
    part = POSITIONS // 4
    date_axis = lax.axis_size("date")
    z = lax.axis_index("date")
    last_row, last_col = routes["last"](lax.axis_index("row"), lax.axis_index("col"))
    z = z.astype(jnp.int32).reshape(1)
    last_row, last_col = last_row.reshape(1), last_col.reshape(1)

    piece_shape = jax.ShapeDtypeStruct((dates, POSITIONS // 2 + part, features), BF16)
    part_shape = jax.ShapeDtypeStruct((dates, part, features), BF16)
    token_shape = jax.ShapeDtypeStruct((8, 128), F32)
    key_columns = -(-(features % 128 + features) // 128) * 128
    tile_bytes = pixels.size * 2

    packed = call(
        pack,
        [piece_shape] * 2 + [part_shape] * 2,
        [VMEM],
        [pltpu.VMEM(pixels.shape[1:], F32)],
        10**10,
        tile_bytes * 2,
        "pack",
    )(pixels)
    low, high, low_right, high_right = (
        lax.ppermute(piece, plane, routes[name])
        for piece, name in zip(packed, ("low", "high", "low_right", "high_right"))
    )
    bias = call(
        bias_kernel,
        jax.ShapeDtypeStruct((heads, POSITIONS, PAIR), F32),
        [VMEM, VMEM],
        [pltpu.VMEM((WINDOW * 32, 128), F32)],
        10**9,
        10**6,
        "position_bias",
    )(bias_network_first, bias_network_second.T)

    projected = [
        pltpu.VMEM((features, token_total), BF16),
        pltpu.VMEM((token_total, key_columns), BF16),
        pltpu.VMEM((token_total, key_columns), BF16),
        pltpu.VMEM((features, token_total), BF16),
        pltpu.VMEM((features, token_total), BF16),
    ]

    weights = (
        window_output_weight,
        feedforward_up_weight,
        feedforward_down_weight.T,
        attention_norm_gain,
        feedforward_norm_gain,
    )
    settle_flops = 2 * token_total * features * (features + 2 * hidden)
    attend_flops = 2 * token_total * features * 3 * features * 2

    def inner_layer(low, high):
        mixed_heads = call(
            inner_attention,
            jax.ShapeDtypeStruct((features, token_total), BF16),
            [VMEM] * 2 + [SMEM] * 2 + [VMEM] * 2,
            projected[:4],
            attend_flops,
            4 * 10**6,
            "inner_attention",
            14,
        )(low, high, last_row, head_logit_scale, bias, window_query_key_value_weight)
        return call(
            inner_settle,
            [part_shape] * 4 + [token_shape],
            [SMEM] + [VMEM] * 8,
            [],
            settle_flops,
            9 * 10**6,
            "inner_settle",
            20,
        )(z, low, high, mixed_heads, *weights)

    def straddle_layer(corners, token):
        return call(
            straddle_window,
            [part_shape] * 4 + [token_shape],
            [SMEM] * 4 + [VMEM] * 4 + [ANY] + [VMEM] * 7,
            projected + [pltpu.VMEM((token_total, features), F32)],
            attend_flops + settle_flops,
            13 * 10**6,
            "straddle_window",
            24,
        )(
            z,
            last_row,
            last_col,
            head_logit_scale,
            *corners,
            token,
            bias,
            window_query_key_value_weight,
            *weights,
        )

    def time_layer(pieces, token):
        return call(
            functools.partial(time_kernel, features // heads),
            [part_shape] * 4 + [token_shape],
            [SMEM, SMEM] + [VMEM] * 4 + [ANY] + [VMEM] * 4,
            projected[:2] + projected[3:],
            2 * token_total * features * 4 * features,
            5 * 10**6,
            "time_layer",
            14,
        )(
            z,
            acquisition_rank,
            *pieces,
            token,
            date_rank_embedding,
            temporal_norm_gain,
            temporal_query_key_value_weight,
            temporal_output_weight,
        )

    def to_dates(pieces, kind):
        return [lax.ppermute(piece, space, routes[kind][k]) for k, piece in enumerate(pieces)]

    def to_home(pieces):
        return [
            piece
            if k == 0
            else lax.ppermute(piece, "date", [(i, (i - k) % date_axis) for i in range(date_axis)])
            for k, piece in enumerate(pieces)
        ]

    *inner, token = inner_layer(low, high)
    inner = to_dates(inner, "inner")
    *straddle, token = straddle_layer([low, high, low_right, high_right], token)
    straddle = to_dates(straddle, "straddle")
    *inner, token = time_layer(inner, token)
    inner = to_home(inner)
    *straddle, token = time_layer(straddle, token)
    straddle = to_home(straddle)
    return call(
        assemble,
        jax.ShapeDtypeStruct(pixels.shape, BF16),
        [SMEM] + [VMEM] * 8,
        [pltpu.VMEM(pixels.shape, F32)],
        0,
        tile_bytes * 2,
        "assemble",
    )(z, *inner, *straddle)


def plan(mesh):
    dates, rows, cols = (mesh.shape[name] for name in ("date", "row", "col"))
    high, low, core = 2, cols // 2, 2
    reach = high * low

    def place(r, c):
        x, y = r // high, (r % high) * low + c // core
        y = (y + 1) % reach
        return x * high + y // low, (y % low) * core + c % core

    def flat(r, c):
        return (r % rows) * cols + c % cols

    def spot(z, r, c):
        return (z % dates) * rows * cols + flat(r, c)

    tiles = [(r, c) for r in range(rows) for c in range(cols)]

    def route(down, right):
        return [(flat(r + down, c + right), flat(*place(r, c))) for r, c in tiles]

    def forward(kind, k):
        pairs = []
        for z in range(dates):
            q = (z + k) % dates
            right = q % 2 if kind == "straddle" else 0
            for r, c in tiles:
                pairs.append((spot(z, *place(r, c)), spot(q, r + q // 2, c + right)))
        return pairs

    def last(row, col):
        y = (row % high) * low + col // core
        y = (y + reach - 1) % reach
        r = (row // high) * high + y // low
        c = (y % low) * core + col % core
        return (r == rows - 1).astype(jnp.int32), (c == cols - 1).astype(jnp.int32)

    return {
        "low": route(0, 0),
        "high": route(1, 0),
        "low_right": route(0, 1),
        "high_right": route(1, 1),
        "inner": [forward("inner", k) for k in range(dates)],
        "straddle": [forward("straddle", k) for k in range(dates)],
        "last": last,
    }


def solution(mesh):
    placed = (P("date", "row", "col", None),) + (P(),) * 14
    return jax.shard_map(
        functools.partial(local, plan(mesh)),
        mesh=mesh,
        in_specs=placed,
        out_specs=P("date", "row", "col", None),
        check_vma=False,
    )
```
